512 devices in a mesh: chan: 128 (over y, z, core), tm: 4 (over x).
Axes of the slice: x: 4, y: 8, z: 8, core: 2. Of those that a mesh axis runs over, the one named last changes fastest.
Arguments:
- samples: float32 [512, 32, 2048], P('chan', 'tm'), may hold values from -6 to 6
- block_owner: int32 [128], replicated, may hold values from 0 to 127, as said below
Outputs:
- correlations: float32 [128, 4, 4, 4, 512], P('chan', None, None, None, 'tm')
The draws below stay inside these ranges and needn't reach their ends.
Inputs may be any that keep to these rules, and one draw needn't show every extreme that they name: block_owner is a permutation that, for each aligned pair of blocks 2i and 2i + 1, either keeps both or swaps them; at least one pair is swapped.
All inputs are finite; a program needn't handle non-finite values.
Results may differ from the reference program's by a relative error of at most 0.0054.
Values may be sent and summed in bfloat16 or wider, within the bound.
A program may use at most 128 MiB of HBM per device.

```python
import math
import jax
import jax.numpy as jnp
from jax import lax

CH_DEV = 4
SEG_DEV = 8
NSEG = 2048
LAGS = 512
SMOOTH = 32
BAND = 4
NF = 1024
CHANNELS = 512
SEGMENTS = 32
N_CHAN = 128
N_TM = 4


def draw_block_owner(key, part):
    key = jax.random.fold_in(key, 11)
    first_key, second_key = jax.random.split(key)
    pairs = N_CHAN // 2
    flips = jax.random.randint(first_key, (pairs,), 0, 2)
    forced = jax.random.randint(second_key, (), 0, pairs)
    flips = jnp.where(jnp.arange(pairs) == forced, 1, flips)
    index = jnp.arange(N_CHAN, dtype=jnp.int32)
    partner = jnp.bitwise_xor(index, 1)
    return jnp.where(flips[index // 2] == 1, partner, index).astype(jnp.int32)


def levels(rng, shape, shards, low, top_value):
    gain = 1.0
    for position, parts in shards:
        steps = jax.random.uniform(jax.random.fold_in(jax.random.fold_in(rng, 6), position), (parts,), jnp.float32, low / len(shards), top_value / len(shards))
        gain = gain * jnp.repeat(jnp.exp(steps), shape[position] // parts).reshape((-1,) + (1,) * (len(shape) - 1 - position))
    return gain


def noise(key, extent, scale, bound, cuts=(), held_as=jnp.bfloat16):
    drawn = jax.random.normal(key, extent, jnp.float32) * scale
    if len(cuts) > 0:
        drawn = levels(key, extent, cuts, -0.22, 0.18) * drawn
    return jnp.clip(drawn, min=-bound, max=bound).astype(held_as)


def setup_inputs(seed: int = 0) -> dict:
    key_of = jax.random.split(jax.random.key(seed), 3)
    samples = noise(key_of[0], (CHANNELS, SEGMENTS, NSEG), 1.0, 6.0, ((0, 128), (1, 4)), jnp.float32)
    block_owner = draw_block_owner(jax.random.fold_in(key_of[2], 71), 0)
    return {"samples": samples, "block_owner": block_owner}


EPSILON = 1e-06

def normalize(real_part, imag_part):
    magnitude = jnp.sqrt(real_part * real_part + imag_part * imag_part)
    lead = len(magnitude.shape) - 1
    width = 2 * SMOOTH + 1
    total = lax.reduce_window(magnitude, jnp.array(0.0, magnitude.dtype), lax.add, (1,) * lead + (width,), (1,) * (lead + 1), ((0, 0),) * lead + ((SMOOTH, SMOOTH),))
    ones = jnp.ones((NF,), magnitude.dtype)
    count = lax.reduce_window(ones, jnp.array(0.0, magnitude.dtype), lax.add, (width,), (1,), ((SMOOTH, SMOOTH),))
    smooth = total / count
    return jnp.concatenate([real_part / (smooth + EPSILON), imag_part / (smooth + EPSILON)], -1).astype(jnp.bfloat16)

def lag_table():
    freq_index = jnp.arange(NF, dtype=jnp.int32)
    lag_index = jnp.arange(LAGS, dtype=jnp.int32) - LAGS // 2
    phase = freq_index[:, None] * lag_index[None, :] % NSEG
    angle = phase.astype(jnp.float32) * (2.0 * math.pi / NSEG)
    factor = 1.0 / math.sqrt(NF)
    return jnp.concatenate([jnp.cos(angle) * factor, -jnp.sin(angle) * factor], 0).astype(jnp.bfloat16)

def pair_product(first, second):
    return jnp.einsum('isk,jsk->ijk', first.astype(jnp.float32), second.astype(jnp.float32))

def cross_block(left, right, factor):
    left_re, left_im = (left[..., :NF], left[..., NF:])
    right_re, right_im = (right[..., :NF], right[..., NF:])
    real_part = pair_product(left_re, right_re) + pair_product(left_im, right_im)
    imag_part = pair_product(left_im, right_re) - pair_product(left_re, right_im)
    joined = jnp.concatenate([real_part, imag_part], -1) * factor
    return joined.astype(jnp.bfloat16).reshape(left.shape[0] * right.shape[0], NSEG)

def reference(samples, block_owner):
    demeaned = samples - lax.optimization_barrier(jnp.mean(samples, axis=-1, keepdims=True))
    spectrum = jnp.fft.rfft(demeaned, axis=-1)[..., :NF]
    white = normalize(jnp.real(spectrum).astype(jnp.float32), jnp.imag(spectrum).astype(jnp.float32))
    table = lag_table()

    def one_row(row):
        left_all = lax.dynamic_slice_in_dim(white, (row * CH_DEV).astype(jnp.int32), CH_DEV, 0)
        results = []
        for offset in range(1, BAND + 1):
            other = jnp.minimum(row + offset, N_CHAN - 1).astype(jnp.int32)
            right_all = lax.dynamic_slice_in_dim(white, (other * CH_DEV).astype(jnp.int32), CH_DEV, 0)
            total = jnp.zeros((CH_DEV * CH_DEV, LAGS), jnp.float32)
            for group in range(N_TM):
                left = left_all[:, group * SEG_DEV:(group + 1) * SEG_DEV]
                right = right_all[:, group * SEG_DEV:(group + 1) * SEG_DEV]
                cross = cross_block(left, right, 1.0 / SEGMENTS)
                total = total + jnp.dot(cross, table, preferred_element_type=jnp.float32)
            total = jnp.where(row + offset < N_CHAN, total, jnp.zeros_like(total))
            results.append(total.reshape(CH_DEV, CH_DEV, LAGS))
        return jnp.stack(results)
    rows = lax.map(one_row, jnp.arange(N_CHAN, dtype=jnp.int32))
    return jnp.zeros_like(rows).at[block_owner].set(rows)
```

```python
import functools
import math

import jax
import jax.numpy as jnp
import ml_dtypes
import numpy as np
from jax import lax
from jax.experimental import pallas as pl
from jax.experimental.pallas import tpu as pltpu
from jax.sharding import PartitionSpec as P

MESH = pl.DeviceIdType.MESH
NSEG = 2048
LAGS = 512
SMOOTH = 32
BAND = 4
NF = 1024
EPSILON = 1e-06
CH = 4
SEG = 8
ROWS = CH * SEG
LANES = 128
TILE = 16
RADIX = 8
POINTS = NSEG // RADIX
BLOCK = ROWS * TILE
PAIR = CH * CH
N_TM = 4


def tables(segments):
    t2 = np.arange(POINTS)
    radix = np.arange(RADIX)
    angle = 2.0 * math.pi * (radix[:, None] * t2[None, :] % NSEG) / NSEG
    twiddle = np.concatenate([np.cos(angle), np.sin(angle)], 0).astype(np.float32)
    angle = 2.0 * math.pi * (t2[:, None] * np.arange(LANES)[None, :] % POINTS) / POINTS
    cos, sin = np.cos(angle), np.sin(angle)
    dft = np.concatenate(
        [np.concatenate([cos, -sin], 1), np.concatenate([sin, cos], 1)], 0
    ).astype(np.float32)
    bins = radix[:, None] + RADIX * np.arange(LANES)[None, :]
    count = np.minimum(bins, SMOOTH) + np.minimum(NF - 1 - bins, SMOOTH) + 1
    share = (1.0 / count).astype(np.float32)
    lag = np.arange(LAGS) - LAGS // 2
    phase = (bins.reshape(-1)[:, None] * lag[None, :]) % NSEG
    angle = phase.astype(np.float32) * np.float32(2.0 * math.pi / NSEG)
    factor = np.float32(1.0 / math.sqrt(NF))
    lags = np.concatenate([np.cos(angle) * factor, -np.sin(angle) * factor], 0)
    lags = lags.astype(ml_dtypes.bfloat16).astype(np.float32) / np.float32(segments)
    return twiddle, dft, share, lags.astype(ml_dtypes.bfloat16)


def shifted(x, by):
    lane = lax.broadcasted_iota(jnp.int32, x.shape, 1)
    if by > 0:
        return jnp.where(lane >= by, pltpu.roll(x, by, 1), 0.0)
    return jnp.where(lane < LANES + by, pltpu.roll(x, LANES + by, 1), 0.0)


def radix_stage(x, twiddle):
    c = math.sqrt(0.5)
    a0, b0 = x[0] + x[4], x[0] - x[4]
    a1, b1 = x[1] + x[5], x[1] - x[5]
    a2, b2 = x[2] + x[6], x[2] - x[6]
    a3, b3 = x[3] + x[7], x[3] - x[7]
    even, odd = a0 + a2, a1 + a3
    low, high = c * (b1 - b3), c * (b1 + b3)
    y = [
        (even + odd, None),
        (b0 + low, -(b2 + high)),
        (a0 - a2, a3 - a1),
        (b0 - low, b2 - high),
        (even - odd, None),
    ]
    y += [(y[3][0], -y[3][1]), (y[2][0], -y[2][1]), (y[1][0], -y[1][1])]
    out = []
    for k1, (re, im) in enumerate(y):
        cos, sin = twiddle[k1 : k1 + 1, :], twiddle[RADIX + k1 : RADIX + k1 + 1, :]
        if k1 == 0:
            out.append((re, jnp.zeros_like(re)))
        elif im is None:
            out.append((re * cos, -(re * sin)))
        else:
            out.append((re * cos + im * sin, im * cos - re * sin))
    return out


def whiten(samples, twiddle, dft, share, z, y, rows):
    x = [samples[:, :, t * POINTS : (t + 1) * POINTS].reshape(ROWS, POINTS) for t in range(RADIX)]
    total = ((x[0] + x[1]) + (x[2] + x[3])) + ((x[4] + x[5]) + (x[6] + x[7]))
    mean = jnp.sum(total, axis=1, keepdims=True) * (1.0 / NSEG)
    x = [part - mean for part in x]
    for k1, (re, im) in enumerate(radix_stage(x, twiddle)):
        z[k1 * ROWS : (k1 + 1) * ROWS, :POINTS] = re
        z[k1 * ROWS : (k1 + 1) * ROWS, POINTS:] = im
    y[...] = jnp.dot(
        z[...], dft[...], precision=lax.Precision.HIGHEST, preferred_element_type=jnp.float32
    )
    re = [y[m * ROWS : (m + 1) * ROWS, :LANES] for m in range(RADIX)]
    im = [y[m * ROWS : (m + 1) * ROWS, LANES:] for m in range(RADIX)]
    size = [jnp.sqrt(r * r + i * i) for r, i in zip(re, im)]
    before, after = [size[0]], [size[-1]]
    for m in range(1, RADIX):
        before.append(before[-1] + size[m])
        after.append(after[-1] + size[RADIX - 1 - m])
    after = after[::-1]
    whole = before[-1]
    middle = whole
    for by in (1, 2, 3):
        middle = middle + (shifted(whole, by) + shifted(whole, -by))
    for m in range(RADIX):
        window = middle + (shifted(before[m], -4) + shifted(after[m], 4))
        scale = 1.0 / (window * share[m : m + 1, :] + EPSILON)
        rows[pl.ds(m, ROWS, stride=TILE), :] = re[m] * scale
        rows[pl.ds(RADIX + m, ROWS, stride=TILE), :] = im[m] * scale


def pair_cross(white, left, right, cross, place):
    def body(s, total):
        def halves(slot, channel):
            start = pl.multiple_of(slot * BLOCK + (channel * SEG + s) * TILE, TILE)
            tile = white[pl.ds(start, TILE), :].astype(jnp.float32)
            return tile[:RADIX, :], tile[RADIX:, :]

        lefts = [halves(left, i) for i in range(CH)]
        rights = [halves(right, j) for j in range(CH)]
        out = []
        for i in range(CH):
            for j in range(CH):
                (lr, li), (rr, ri) = lefts[i], rights[j]
                re, im = total[2 * (i * CH + j)], total[2 * (i * CH + j) + 1]
                out.append(re + (lr * rr + li * ri))
                out.append(im + (li * rr - lr * ri))
        return tuple(out)

    zero = jnp.zeros((RADIX, LANES), jnp.float32)
    total = lax.fori_loop(0, SEG, body, (zero,) * (2 * PAIR))
    for p in range(PAIR):
        start = (place * PAIR + p) * TILE
        cross[start : start + RADIX, :] = total[2 * p]
        cross[start + RADIX : start + TILE, :] = total[2 * p + 1]


def kernel(
    chips, samples_ref, owner_ref, twiddle_ref, dft_ref, share_ref, lags_ref, out_ref,
    samples, twiddle, dft, share, lags, z, y, rows, white, cross, result,
    from_a, from_x, from_b, from_y,
    load_sem, send_sem, recv_sem, sum_send, sum_recv,
):
    position, t = lax.axis_index("chan"), lax.axis_index("tm")
    q, e = position // 2, lax.rem(position, 2)
    after, before = lax.rem(q + 1, chips), lax.rem(q + chips - 1, chips)

    def device(chip, core, row):
        return (chip * 2 + core, row)

    def other(step):
        return lax.rem(t + step, N_TM)

    barrier = pltpu.get_barrier_semaphore()

    def greet(target):
        pl.semaphore_signal(barrier, inc=1, device_id=target, device_id_type=MESH)

    greet(device(q, 1 - e, t))
    greet(device(before, e, t))
    for core in (0, 1):
        greet(device(after, core, t))
        for step in range(1, N_TM):
            greet(device(q, core, other(step)))
            greet(device(after, core, other(step)))

    loads = [
        pltpu.make_async_copy(src, dst, load_sem.at[n])
        for n, (src, dst) in enumerate(
            [(samples_ref, samples), (twiddle_ref, twiddle), (dft_ref, dft), (share_ref, share),
             (lags_ref, lags)]
        )
    ]
    for load in loads:
        load.start()
    for load in loads[:4]:
        load.wait()

    whiten(samples, twiddle, dft, share, z, y, rows)
    own = pl.ds(pl.multiple_of(e * BLOCK, BLOCK), BLOCK)
    white[own, :] = rows[...].astype(jnp.bfloat16)

    pl.semaphore_wait(barrier, 2 + 2 + 4 * (N_TM - 1))

    def send(slot, n, target):
        place = pl.ds(pl.multiple_of(slot * BLOCK, BLOCK), BLOCK)
        return pltpu.make_async_remote_copy(
            src_ref=white.at[own, :], dst_ref=white.at[place, :], send_sem=send_sem.at[n],
            recv_sem=recv_sem.at[n], device_id=target, device_id_type=MESH,
        )

    copies = [
        send(4, 0, device(before, e, t)),
        send(2 + e, 1, device(after, e, t)),
        send(e, 2, device(q, 1 - e, t)),
    ]
    for copy in copies:
        copy.start()
    passed = pl.ds(3 * BLOCK, BLOCK)
    pass_on = pltpu.make_async_remote_copy(
        src_ref=white.at[passed, :], dst_ref=white.at[passed, :], send_sem=send_sem.at[3],
        recv_sem=recv_sem.at[3], device_id=device(q, 1 - e, t), device_id_type=MESH,
    )
    for copy in copies:
        copy.wait_recv()

    @pl.when(e == 1)
    def _():
        pass_on.start()

    pair_cross(white, 0, 4, cross, 0)
    pair_cross(white, 1, 4, cross, 1)
    pair_cross(white, 2 * (1 - e), 4 - 3 * e, cross, 2)

    @pl.when(e == 0)
    def _():
        pass_on.wait_recv()

    pair_cross(white, 3, 4, cross, 3)

    loads[4].wait()
    parts = [
        cross[pl.ds(n, BAND * PAIR, stride=TILE), :].astype(jnp.bfloat16) for n in range(TILE)
    ]
    corr = jnp.dot(
        jnp.concatenate(parts, axis=1), lags[...], preferred_element_type=jnp.float32
    )

    swap = owner_ref[2 * q] != 2 * q
    swap_before = owner_ref[2 * before] != 2 * before
    r = [corr[n * PAIR : (n + 1) * PAIR, :] for n in range(BAND)]
    first = jnp.where(swap, r[1], r[0])
    second = jnp.where(swap, r[0], r[1])

    def put(place, value):
        for row in range(N_TM):
            result[row, place * PAIR : (place + 1) * PAIR, :] = value[
                :, row * LANES : (row + 1) * LANES
            ]

    put(0, first)

    @pl.when(e == 0)
    def _():
        put(1, second)
        put(2, jnp.where(swap_before, r[3], r[2]))
        put(3, jnp.where(swap_before, r[2], r[3]))

    @pl.when(e == 1)
    def _():
        put(1, r[2])
        put(2, second)
        put(3, r[3])

    def handed(core, step):
        row = other(step)
        if core == 0:
            plan = [(0, 1, from_a, 0), (1, 1, from_a, 0), (2, 1, from_b, 2), (3, 1, from_b, 2)]
        else:
            plan = [(0, 2, from_x, 1), (1, 2, from_x, 1), (3, 1, from_y, 3), (3, 1, from_y, 3)]
        sends = []
        for n, (place, size, buffer, kind) in enumerate(plan):
            if n < 2 and step == 0 and n == core:
                continue
            sends.append(
                pltpu.make_async_remote_copy(
                    src_ref=result.at[row, pl.ds(place * PAIR, size * PAIR), :],
                    dst_ref=buffer.at[t],
                    send_sem=sum_send.at[step, n],
                    recv_sem=sum_recv.at[kind, t],
                    device_id=device(q if n < 2 else before, n % 2, row),
                    device_id_type=MESH,
                )
            )
        return sends

    for core in (0, 1):

        @pl.when(e == core)
        def _():
            sends = []
            for step in (2, 1, 3, 0):
                sends += handed(core, step)
            for copy in sends:
                copy.start()
            if core == 0:
                from_a[t] = result[t, :PAIR, :]
            else:
                from_x[t] = result[t, PAIR : 3 * PAIR, :]
            for copy in sends:
                copy.wait_send()

    def arrived(size, buffer, n, row):
        return pltpu.make_async_remote_copy(
            src_ref=result.at[0, pl.ds(0, size), :], dst_ref=buffer.at[row],
            send_sem=sum_send.at[0, n], recv_sem=sum_recv.at[n, row],
            device_id=device(q, 1 - e, t), device_id_type=MESH,
        )

    for step in range(N_TM):
        row = other(step)
        if step > 0:
            arrived(PAIR, from_a, 0, row).wait_recv()
            arrived(2 * PAIR, from_x, 1, row).wait_recv()
        arrived(PAIR, from_b, 2, row).wait_recv()
        arrived(PAIR, from_y, 3, row).wait_recv()

    @pl.when(e == 1)
    def _():
        arrived(PAIR, from_a, 0, t).wait_recv()

    @pl.when(e == 0)
    def _():
        arrived(2 * PAIR, from_x, 1, t).wait_recv()

    def summed(buffer):
        return (buffer[0] + buffer[1]) + (buffer[2] + buffer[3])

    a, x, b, last = summed(from_a), summed(from_x), summed(from_b), summed(from_y)
    flip = e == 1
    right = jnp.where(flip, x[PAIR:], x[:PAIR])
    inner = jnp.where(flip, x[:PAIR], x[PAIR:])
    odd = jnp.logical_xor(swap, e == 1)
    block = 2 * q + odd.astype(jnp.int32)
    low = [inner, a, right, b]
    high = [a, right, b, last]
    for n in range(BAND):
        value = jnp.where(odd, high[n], low[n])
        out_ref[n * PAIR : (n + 1) * PAIR, :] = jnp.where(
            block + n + 1 < 2 * chips, value, jnp.zeros_like(value)
        )

    for copy in copies:
        copy.wait_send()

    @pl.when(e == 1)
    def _():
        pass_on.wait_send()


def shards(chips, samples, block_owner):
    segments = samples.shape[1] * N_TM
    twiddle, dft, share, lags = tables(segments)
    anywhere = pl.BlockSpec(memory_space=pl.ANY)
    out = pl.pallas_call(
        functools.partial(kernel, chips),
        out_shape=jax.ShapeDtypeStruct((BAND * PAIR, LANES), jnp.float32),
        in_specs=[anywhere, pl.BlockSpec(memory_space=pltpu.SMEM)] + [anywhere] * 4,
        out_specs=pl.BlockSpec(memory_space=pltpu.VMEM),
        scratch_shapes=[
            pltpu.VMEM((CH, SEG, NSEG), jnp.float32),
            pltpu.VMEM(twiddle.shape, jnp.float32),
            pltpu.VMEM(dft.shape, jnp.float32),
            pltpu.VMEM(share.shape, jnp.float32),
            pltpu.VMEM(lags.shape, jnp.bfloat16),
            pltpu.VMEM((RADIX * ROWS, 2 * POINTS), jnp.float32),
            pltpu.VMEM((RADIX * ROWS, 2 * LANES), jnp.float32),
            pltpu.VMEM((BLOCK, LANES), jnp.float32),
            pltpu.VMEM((5 * BLOCK, LANES), jnp.bfloat16),
            pltpu.VMEM((BAND * PAIR * TILE, LANES), jnp.float32),
            pltpu.VMEM((N_TM, BAND * PAIR, LANES), jnp.float32),
            pltpu.VMEM((N_TM, PAIR, LANES), jnp.float32),
            pltpu.VMEM((N_TM, 2 * PAIR, LANES), jnp.float32),
            pltpu.VMEM((N_TM, PAIR, LANES), jnp.float32),
            pltpu.VMEM((N_TM, PAIR, LANES), jnp.float32),
            pltpu.SemaphoreType.DMA((5,)),
            pltpu.SemaphoreType.DMA((4,)),
            pltpu.SemaphoreType.DMA((4,)),
            pltpu.SemaphoreType.DMA((N_TM, 4)),
            pltpu.SemaphoreType.DMA((4, N_TM)),
        ],
        compiler_params=pltpu.CompilerParams(
            collective_id=0, has_side_effects=True, vmem_limit_bytes=32 * 1024 * 1024
        ),
    )(
        samples, block_owner, jnp.asarray(twiddle), jnp.asarray(dft), jnp.asarray(share),
        jnp.asarray(lags),
    )
    return out.reshape(1, BAND, CH, CH, LANES)


def solution(mesh):
    in_specs = (P("chan", "tm", None), P())
    out_specs = P("chan", None, None, None, "tm")
    chips = mesh.shape["chan"] // 2
    return jax.shard_map(
        functools.partial(shards, chips), mesh=mesh, in_specs=in_specs, out_specs=out_specs,
        check_vma=False,
    )
```

```python
import functools
import math

import jax
import jax.numpy as jnp
import ml_dtypes
import numpy as np
from jax import lax
from jax.experimental import pallas as pl
from jax.experimental.pallas import tpu as pltpu
from jax.sharding import PartitionSpec as P

MESH = pl.DeviceIdType.MESH
NSEG = 2048
LAGS = 512
SMOOTH = 32
BAND = 4
NF = 1024
EPSILON = 1e-06
CH = 4
SEG = 8
ROWS = CH * SEG
LANES = 128
TILE = 16
RADIX = 8
POINTS = NSEG // RADIX
BLOCK = ROWS * TILE
PAIR = CH * CH
N_TM = 4


def tables(segments):
    t2 = np.arange(POINTS)
    radix = np.arange(RADIX)
    angle = 2.0 * math.pi * (radix[:, None] * t2[None, :] % NSEG) / NSEG
    twiddle = np.concatenate([np.cos(angle), np.sin(angle)], 0).astype(np.float32)
    angle = 2.0 * math.pi * (t2[:, None] * np.arange(LANES)[None, :] % POINTS) / POINTS
    cos, sin = np.cos(angle), np.sin(angle)
    dft = np.concatenate(
        [np.concatenate([cos, -sin], 1), np.concatenate([sin, cos], 1)], 0
    ).astype(np.float32)
    bins = radix[:, None] + RADIX * np.arange(LANES)[None, :]
    count = np.minimum(bins, SMOOTH) + np.minimum(NF - 1 - bins, SMOOTH) + 1
    share = (1.0 / count).astype(np.float32)
    angle = 2.0 * math.pi * (np.arange(LANES)[:, None] * np.arange(POINTS)[None, :] % POINTS) / POINTS
    cos, sin = np.cos(angle), np.sin(angle)
    inner = np.concatenate([np.concatenate([cos, sin], 1), np.concatenate([-sin, cos], 1)], 0)
    lag = np.arange(LAGS) - LAGS // 2
    angle = 2.0 * math.pi * (radix[:, None] * lag[None, :] % NSEG) / NSEG
    factor = 1.0 / (math.sqrt(NF) * segments)
    outer = np.concatenate([np.cos(angle), np.sin(angle)], 0) * factor
    return twiddle, dft, share, inner.astype(ml_dtypes.bfloat16), outer.astype(np.float32)


def shifted(x, by):
    lane = lax.broadcasted_iota(jnp.int32, x.shape, 1)
    if by > 0:
        return jnp.where(lane >= by, pltpu.roll(x, by, 1), 0.0)
    return jnp.where(lane < LANES + by, pltpu.roll(x, LANES + by, 1), 0.0)


def radix_stage(x, twiddle):
    c = math.sqrt(0.5)
    a0, b0 = x[0] + x[4], x[0] - x[4]
    a1, b1 = x[1] + x[5], x[1] - x[5]
    a2, b2 = x[2] + x[6], x[2] - x[6]
    a3, b3 = x[3] + x[7], x[3] - x[7]
    even, odd = a0 + a2, a1 + a3
    low, high = c * (b1 - b3), c * (b1 + b3)
    y = [
        (even + odd, None),
        (b0 + low, -(b2 + high)),
        (a0 - a2, a3 - a1),
        (b0 - low, b2 - high),
        (even - odd, None),
    ]
    y += [(y[3][0], -y[3][1]), (y[2][0], -y[2][1]), (y[1][0], -y[1][1])]
    out = []
    for k1, (re, im) in enumerate(y):
        cos, sin = twiddle[k1 : k1 + 1, :], twiddle[RADIX + k1 : RADIX + k1 + 1, :]
        if k1 == 0:
            out.append((re, jnp.zeros_like(re)))
        elif im is None:
            out.append((re * cos, -(re * sin)))
        else:
            out.append((re * cos + im * sin, im * cos - re * sin))
    return out


def whiten(samples, twiddle, dft, share, z, y, rows):
    x = [samples[:, :, t * POINTS : (t + 1) * POINTS].reshape(ROWS, POINTS) for t in range(RADIX)]
    total = ((x[0] + x[1]) + (x[2] + x[3])) + ((x[4] + x[5]) + (x[6] + x[7]))
    mean = jnp.sum(total, axis=1, keepdims=True) * (1.0 / NSEG)
    x = [part - mean for part in x]
    for k1, (re, im) in enumerate(radix_stage(x, twiddle)):
        z[k1 * ROWS : (k1 + 1) * ROWS, :POINTS] = re
        z[k1 * ROWS : (k1 + 1) * ROWS, POINTS:] = im
    y[...] = jnp.dot(
        z[...], dft[...], precision=lax.Precision.HIGHEST, preferred_element_type=jnp.float32
    )
    re = [y[m * ROWS : (m + 1) * ROWS, :LANES] for m in range(RADIX)]
    im = [y[m * ROWS : (m + 1) * ROWS, LANES:] for m in range(RADIX)]
    size = [jnp.sqrt(r * r + i * i) for r, i in zip(re, im)]
    before, after = [size[0]], [size[-1]]
    for m in range(1, RADIX):
        before.append(before[-1] + size[m])
        after.append(after[-1] + size[RADIX - 1 - m])
    after = after[::-1]
    whole = before[-1]
    middle = whole
    for by in (1, 2, 3):
        middle = middle + (shifted(whole, by) + shifted(whole, -by))
    for m in range(RADIX):
        window = middle + (shifted(before[m], -4) + shifted(after[m], 4))
        scale = 1.0 / (window * share[m : m + 1, :] + EPSILON)
        rows[pl.ds(m, ROWS, stride=TILE), :] = re[m] * scale
        rows[pl.ds(RADIX + m, ROWS, stride=TILE), :] = im[m] * scale


def pair_cross(white, left, right, cross):
    def body(s, total):
        def halves(slot, channel):
            start = pl.multiple_of(slot * BLOCK + (channel * SEG + s) * TILE, TILE)
            tile = white[pl.ds(start, TILE), :].astype(jnp.float32)
            return tile[:RADIX, :], tile[RADIX:, :]

        lefts = [halves(left, i) for i in range(CH)]
        rights = [halves(right, j) for j in range(CH)]
        out = []
        for i in range(CH):
            for j in range(CH):
                (lr, li), (rr, ri) = lefts[i], rights[j]
                re, im = total[2 * (i * CH + j)], total[2 * (i * CH + j) + 1]
                out.append(re + (lr * rr + li * ri))
                out.append(im + (li * rr - lr * ri))
        return tuple(out)

    zero = jnp.zeros((RADIX, LANES), jnp.float32)
    total = lax.fori_loop(0, SEG, body, (zero,) * (2 * PAIR))
    for p in range(PAIR):
        cross[p * RADIX : (p + 1) * RADIX, :] = total[2 * p]
        cross[(PAIR + p) * RADIX : (PAIR + p + 1) * RADIX, :] = total[2 * p + 1]


def pair_lags(white, left, right, cross, inner, outer):
    pair_cross(white, left, right, cross)
    re = [cross[pl.ds(m, PAIR, stride=RADIX), :] for m in range(RADIX)]
    im = [cross[pl.ds(PAIR * RADIX + m, PAIR, stride=RADIX), :] for m in range(RADIX)]
    parts = [jnp.concatenate(re, axis=0), jnp.concatenate(im, axis=0)]
    spread = jnp.dot(
        jnp.concatenate(parts, axis=1).astype(jnp.bfloat16),
        inner[...],
        preferred_element_type=jnp.float32,
    )
    out = []
    for row in range(N_TM):
        total = None
        for m in range(RADIX):
            lanes = slice(row * LANES, (row + 1) * LANES)
            at = row % 2 * LANES
            re = spread[m * PAIR : (m + 1) * PAIR, at : at + LANES]
            im = spread[m * PAIR : (m + 1) * PAIR, POINTS + at : POINTS + at + LANES]
            term = re * outer[m : m + 1, lanes] - im * outer[RADIX + m : RADIX + m + 1, lanes]
            total = term if total is None else total + term
        out.append(total)
    return out


def kernel(
    chips, samples_ref, owner_ref, twiddle_ref, dft_ref, share_ref, inner_ref, outer_ref, out_ref,
    samples, twiddle, dft, share, inner, outer, owner, z, y, rows, white, cross, result,
    from_a, from_x, from_b, from_y,
    load_sem, send_sem, recv_sem, sum_send, sum_recv, ready,
):
    position, t = lax.axis_index("chan"), lax.axis_index("tm")
    q, e = position // 2, lax.rem(position, 2)
    after, before = lax.rem(q + 1, chips), lax.rem(q + chips - 1, chips)

    def device(chip, core, row):
        return (chip * 2 + core, row)

    def other(step):
        return lax.rem(t + step, N_TM)

    barrier = pltpu.get_barrier_semaphore()

    def greet(target):
        pl.semaphore_signal(barrier, inc=1, device_id=target, device_id_type=MESH)

    has_before, has_after = q > 0, q < chips - 1

    @pl.when(has_before)
    def _():
        greet(device(before, 1, t))

    @pl.when(jnp.logical_and(has_before, e == 0))
    def _():
        greet(device(before, 0, t))

    greet(device(q, 1 - e, t))
    for step in range(1, N_TM):
        for core in (0, 1):
            greet(device(q, core, other(step)))

    loads = [
        pltpu.make_async_copy(src, dst, load_sem.at[n])
        for n, (src, dst) in enumerate(
            [(samples_ref, samples), (twiddle_ref, twiddle), (dft_ref, dft), (share_ref, share),
             (inner_ref, inner), (outer_ref, outer), (owner_ref, owner)]
        )
    ]
    for load in loads:
        load.start()
    last = q // (chips - 1)
    pl.semaphore_wait(barrier, 1 + 2 * (N_TM - 1) + (1 - last) * (1 + e))

    @pl.when(has_after)
    def _():
        pl.semaphore_signal(ready, inc=1, device_id=device(after, e, t), device_id_type=MESH)

    for load in loads[:4]:
        load.wait()

    whiten(samples, twiddle, dft, share, z, y, rows)
    own = pl.ds(pl.multiple_of(e * BLOCK, BLOCK), BLOCK)
    white[own, :] = rows[...].astype(jnp.bfloat16)

    def send(slot, n, target):
        place = pl.ds(pl.multiple_of(slot * BLOCK, BLOCK), BLOCK)
        return pltpu.make_async_remote_copy(
            src_ref=white.at[own, :], dst_ref=white.at[place, :], send_sem=send_sem.at[n],
            recv_sem=recv_sem.at[n], device_id=target, device_id_type=MESH,
        )

    to_after = send(2 + e, 1, device(after, e, t))
    to_after_other = send(3, 3, device(after, 0, t))
    to_other = send(e, 2, device(q, 1 - e, t))
    to_before = send(4, 0, device(before, e, t))

    def put(place, value):
        for row in range(N_TM):
            result[row, place * PAIR : (place + 1) * PAIR, :] = value[row]

    def chosen(by, yes, no):
        return [jnp.where(by, a, b) for a, b in zip(yes, no)]

    def lagged(left, right):
        return pair_lags(white, left, right, cross, inner, outer)

    def hand(core, step, n):
        row = other(step)
        if core == 0:
            place, size, buffer, kind = n, 1, (from_a, from_b)[n // 2], n // 2 * 2
        else:
            place, size = (0, 1, 3, 3)[n], 2 - n // 2
            buffer, kind = (from_x, from_y)[n // 2], 1 + n // 2 * 2
        return pltpu.make_async_remote_copy(
            src_ref=result.at[row, pl.ds(place * PAIR, size * PAIR), :],
            dst_ref=buffer.at[t],
            send_sem=sum_send.at[step, n],
            recv_sem=sum_recv.at[kind, t],
            device_id=device(q if n < 2 else before, n % 2, row),
            device_id_type=MESH,
        )

    def hands(core, targets):
        return [
            hand(core, step, n)
            for step in (2, 1, 3, 0)
            for n in targets
            if step > 0 or n != core
        ]

    def start(copies):
        for copy in copies:
            copy.start()
        return copies

    loads[4].wait()
    loads[5].wait()
    loads[6].wait()
    swap = owner[2 * q] != 2 * q
    swap_before = owner[2 * before] != 2 * before

    to_other.start()

    @pl.when(has_after)
    def _():
        @pl.when(e == 1)
        def _():
            to_after_other.start()

        to_after.start()

    @pl.when(has_before)
    def _():
        pl.semaphore_wait(ready, 1)
        to_before.start()

    to_other.wait_recv()

    @pl.when(e == 0)
    def _():
        @pl.when(has_after)
        def _():
            to_before.wait_recv()

        one, two = lagged(0, 4), lagged(1, 4)
        put(0, chosen(swap, two, one))
        put(1, chosen(swap, one, two))
        near = start(hands(0, (0, 1)))
        from_a[t] = result[t, :PAIR, :]

        @pl.when(has_before)
        def _():
            to_after.wait_recv()
            to_after_other.wait_recv()
            one, two = lagged(2, 4), lagged(3, 4)
            put(2, chosen(swap_before, two, one))
            put(3, chosen(swap_before, one, two))
            for copy in start(hands(0, (2, 3))):
                copy.wait_send()

        for copy in near:
            copy.wait_send()

    @pl.when(e == 1)
    def _():
        put(1, lagged(0, 1))

        @pl.when(has_after)
        def _():
            to_before.wait_recv()

        one, two = lagged(0, 4), lagged(1, 4)
        put(0, chosen(swap, two, one))
        put(2, chosen(swap, one, two))
        near = start(hands(1, (0, 1)))
        from_x[t] = result[t, PAIR : 3 * PAIR, :]

        @pl.when(has_before)
        def _():
            to_after.wait_recv()
            put(3, lagged(3, 4))
            for copy in start(hands(1, (2, 3))):
                copy.wait_send()

        for copy in near:
            copy.wait_send()

    def arrived(size, buffer, n, row):
        return pltpu.make_async_remote_copy(
            src_ref=result.at[0, pl.ds(0, size), :], dst_ref=buffer.at[row],
            send_sem=sum_send.at[0, n], recv_sem=sum_recv.at[n, row],
            device_id=device(q, 1 - e, t), device_id_type=MESH,
        )

    for step in range(N_TM):
        row = other(step)
        if step > 0:
            arrived(PAIR, from_a, 0, row).wait_recv()
            arrived(2 * PAIR, from_x, 1, row).wait_recv()

    @pl.when(has_after)
    def _():
        for row in range(N_TM):
            arrived(PAIR, from_b, 2, row).wait_recv()
            arrived(PAIR, from_y, 3, row).wait_recv()

    @pl.when(e == 1)
    def _():
        arrived(PAIR, from_a, 0, t).wait_recv()

    @pl.when(e == 0)
    def _():
        arrived(2 * PAIR, from_x, 1, t).wait_recv()

    def summed(buffer):
        return (buffer[0] + buffer[1]) + (buffer[2] + buffer[3])

    a, x, b, last = summed(from_a), summed(from_x), summed(from_b), summed(from_y)
    flip = e == 1
    right = jnp.where(flip, x[PAIR:], x[:PAIR])
    inner = jnp.where(flip, x[:PAIR], x[PAIR:])
    odd = jnp.logical_xor(swap, e == 1)
    block = 2 * q + odd.astype(jnp.int32)
    low = [inner, a, right, b]
    high = [a, right, b, last]
    for n in range(BAND):
        value = jnp.where(odd, high[n], low[n])
        out_ref[n * PAIR : (n + 1) * PAIR, :] = jnp.where(
            block + n + 1 < 2 * chips, value, jnp.zeros_like(value)
        )

    to_other.wait_send()

    @pl.when(has_before)
    def _():
        to_before.wait_send()

    @pl.when(has_after)
    def _():
        to_after.wait_send()

        @pl.when(e == 1)
        def _():
            to_after_other.wait_send()


def shards(chips, samples, block_owner):
    segments = samples.shape[1] * N_TM
    twiddle, dft, share, inner, outer = tables(segments)
    stay = pl.BlockSpec(memory_space=pltpu.HBM)
    out = pl.pallas_call(
        functools.partial(kernel, chips),
        out_shape=jax.ShapeDtypeStruct((BAND * PAIR, LANES), jnp.float32),
        in_specs=[stay] * 7,
        out_specs=pl.BlockSpec(memory_space=pltpu.VMEM),
        scratch_shapes=[
            pltpu.VMEM((CH, SEG, NSEG), jnp.float32),
            pltpu.VMEM(twiddle.shape, jnp.float32),
            pltpu.VMEM(dft.shape, jnp.float32),
            pltpu.VMEM(share.shape, jnp.float32),
            pltpu.VMEM(inner.shape, jnp.bfloat16),
            pltpu.VMEM(outer.shape, jnp.float32),
            pltpu.SMEM(block_owner.shape, jnp.int32),
            pltpu.VMEM((RADIX * ROWS, 2 * POINTS), jnp.float32),
            pltpu.VMEM((RADIX * ROWS, 2 * LANES), jnp.float32),
            pltpu.VMEM((BLOCK, LANES), jnp.float32),
            pltpu.VMEM((5 * BLOCK, LANES), jnp.bfloat16),
            pltpu.VMEM((2 * PAIR * RADIX, LANES), jnp.float32),
            pltpu.VMEM((N_TM, BAND * PAIR, LANES), jnp.float32),
            pltpu.VMEM((N_TM, PAIR, LANES), jnp.float32),
            pltpu.VMEM((N_TM, 2 * PAIR, LANES), jnp.float32),
            pltpu.VMEM((N_TM, PAIR, LANES), jnp.float32),
            pltpu.VMEM((N_TM, PAIR, LANES), jnp.float32),
            pltpu.SemaphoreType.DMA((7,)),
            pltpu.SemaphoreType.DMA((4,)),
            pltpu.SemaphoreType.DMA((4,)),
            pltpu.SemaphoreType.DMA((N_TM, 4)),
            pltpu.SemaphoreType.DMA((4, N_TM)),
            pltpu.SemaphoreType.REGULAR,
        ],
        compiler_params=pltpu.CompilerParams(collective_id=0, has_side_effects=True),
    )(
        samples, block_owner, jnp.asarray(twiddle), jnp.asarray(dft), jnp.asarray(share),
        jnp.asarray(inner), jnp.asarray(outer),
    )
    return out.reshape(1, BAND, CH, CH, LANES)


def solution(mesh):
    in_specs = (P("chan", "tm", None), P())
    out_specs = P("chan", None, None, None, "tm")
    chips = mesh.shape["chan"] // 2
    return jax.shard_map(
        functools.partial(shards, chips), mesh=mesh, in_specs=in_specs, out_specs=out_specs,
        check_vma=False,
    )
```

```python
import functools
import math

import jax
import jax.numpy as jnp
import ml_dtypes
import numpy as np
from jax import lax
from jax.experimental import pallas as pl
from jax.experimental.pallas import tpu as pltpu
from jax.sharding import PartitionSpec as P

MESH = pl.DeviceIdType.MESH
NSEG = 2048
LAGS = 512
SMOOTH = 32
BAND = 4
NF = 1024
EPSILON = 1e-06
CH = 4
SEG = 8
ROWS = CH * SEG
LANES = 128
TILE = 16
RADIX = 8
POINTS = NSEG // RADIX
BLOCK = ROWS * TILE
PAIR = CH * CH
N_TM = 4
ROW = 8


def tables(segments):
    t2 = np.arange(POINTS)
    radix = np.arange(RADIX)
    angle = 2.0 * math.pi * (radix[:, None] * t2[None, :] % NSEG) / NSEG
    twiddle = np.concatenate([np.cos(angle), np.sin(angle)], 0).astype(np.float32)
    angle = 2.0 * math.pi * (t2[:, None] * np.arange(LANES)[None, :] % POINTS) / POINTS
    cos, sin = np.cos(angle), np.sin(angle)
    dft = np.concatenate(
        [np.concatenate([cos, -sin], 1), np.concatenate([sin, cos], 1)], 0
    ).astype(np.float32)
    bins = radix[:, None] + RADIX * np.arange(LANES)[None, :]
    count = np.minimum(bins, SMOOTH) + np.minimum(NF - 1 - bins, SMOOTH) + 1
    share = (1.0 / count).astype(np.float32)
    angle = 2.0 * math.pi * (np.arange(LANES)[:, None] * np.arange(POINTS)[None, :] % POINTS) / POINTS
    cos, sin = np.cos(angle), np.sin(angle)
    inner = np.concatenate([np.concatenate([cos, sin], 1), np.concatenate([-sin, cos], 1)], 0)
    lag = np.arange(LAGS) - LAGS // 2
    angle = 2.0 * math.pi * (radix[:, None] * lag[None, :] % NSEG) / NSEG
    factor = 1.0 / (math.sqrt(NF) * segments)
    outer = np.concatenate([np.cos(angle), np.sin(angle)], 0) * factor
    return twiddle, dft, share, inner.astype(ml_dtypes.bfloat16), outer.astype(np.float32)


def shifted(x, by):
    lane = lax.broadcasted_iota(jnp.int32, x.shape, 1)
    if by > 0:
        return jnp.where(lane >= by, pltpu.roll(x, by, 1), 0.0)
    return jnp.where(lane < LANES + by, pltpu.roll(x, LANES + by, 1), 0.0)


def radix_stage(x, twiddle):
    c = math.sqrt(0.5)
    a0, b0 = x[0] + x[4], x[0] - x[4]
    a1, b1 = x[1] + x[5], x[1] - x[5]
    a2, b2 = x[2] + x[6], x[2] - x[6]
    a3, b3 = x[3] + x[7], x[3] - x[7]
    even, odd = a0 + a2, a1 + a3
    low, high = c * (b1 - b3), c * (b1 + b3)
    y = [
        (even + odd, None),
        (b0 + low, -(b2 + high)),
        (a0 - a2, a3 - a1),
        (b0 - low, b2 - high),
        (even - odd, None),
    ]
    y += [(y[3][0], -y[3][1]), (y[2][0], -y[2][1]), (y[1][0], -y[1][1])]
    out = []
    for k1, (re, im) in enumerate(y):
        cos, sin = twiddle[k1 : k1 + 1, :], twiddle[RADIX + k1 : RADIX + k1 + 1, :]
        if k1 == 0:
            out.append((re, jnp.zeros_like(re)))
        elif im is None:
            out.append((re * cos, -(re * sin)))
        else:
            out.append((re * cos + im * sin, im * cos - re * sin))
    return out


def whiten(samples, twiddle, dft, share, z, y, rows):
    x = [samples[:, :, t * POINTS : (t + 1) * POINTS].reshape(ROWS, POINTS) for t in range(RADIX)]
    total = ((x[0] + x[1]) + (x[2] + x[3])) + ((x[4] + x[5]) + (x[6] + x[7]))
    mean = jnp.sum(total, axis=1, keepdims=True) * (1.0 / NSEG)
    x = [part - mean for part in x]
    for k1, (re, im) in enumerate(radix_stage(x, twiddle)):
        z[k1 * ROWS : (k1 + 1) * ROWS, :POINTS] = re
        z[k1 * ROWS : (k1 + 1) * ROWS, POINTS:] = im
    y[...] = jnp.dot(
        z[...], dft[...], precision=lax.Precision.HIGHEST, preferred_element_type=jnp.float32
    )
    re = [y[m * ROWS : (m + 1) * ROWS, :LANES] for m in range(RADIX)]
    im = [y[m * ROWS : (m + 1) * ROWS, LANES:] for m in range(RADIX)]
    size = [jnp.sqrt(r * r + i * i) for r, i in zip(re, im)]
    before, after = [size[0]], [size[-1]]
    for m in range(1, RADIX):
        before.append(before[-1] + size[m])
        after.append(after[-1] + size[RADIX - 1 - m])
    after = after[::-1]
    whole = before[-1]
    middle = whole
    for by in (1, 2, 3):
        middle = middle + (shifted(whole, by) + shifted(whole, -by))
    for m in range(RADIX):
        window = middle + (shifted(before[m], -4) + shifted(after[m], 4))
        scale = 1.0 / (window * share[m : m + 1, :] + EPSILON)
        rows[pl.ds(m, ROWS, stride=TILE), :] = re[m] * scale
        rows[pl.ds(RADIX + m, ROWS, stride=TILE), :] = im[m] * scale


def pair_cross(white, left, right, cross, place):
    def body(s, total):
        def halves(slot, channel):
            start = pl.multiple_of(slot * BLOCK + (channel * SEG + s) * TILE, TILE)
            tile = white[pl.ds(start, TILE), :].astype(jnp.float32)
            return tile[:RADIX, :], tile[RADIX:, :]

        lefts = [halves(left, i) for i in range(CH)]
        rights = [halves(right, j) for j in range(CH)]
        out = []
        for i in range(CH):
            for j in range(CH):
                (lr, li), (rr, ri) = lefts[i], rights[j]
                re, im = total[2 * (i * CH + j)], total[2 * (i * CH + j) + 1]
                out.append(re + (lr * rr + li * ri))
                out.append(im + (li * rr - lr * ri))
        return tuple(out)

    zero = jnp.zeros((RADIX, LANES), jnp.float32)
    total = lax.fori_loop(0, SEG, body, (zero,) * (2 * PAIR), unroll=True)
    for p in range(PAIR):
        for part in (0, 1):
            start = ((2 * place + part) * PAIR + p) * RADIX
            cross[start : start + RADIX, :] = total[2 * p + part]


def pair_lags(white, pairs, cross, inner, outer):
    for place, (left, right) in enumerate(pairs):
        pair_cross(white, left, right, cross, place)
    parts = []
    for part in (0, 1):
        rows = [
            cross[pl.ds((2 * place + part) * PAIR * RADIX + m, PAIR, stride=RADIX), :]
            for m in range(RADIX)
            for place in range(len(pairs))
        ]
        parts.append(jnp.concatenate(rows, axis=0))
    spread = jnp.dot(
        jnp.concatenate(parts, axis=1).astype(jnp.bfloat16),
        inner[...],
        preferred_element_type=jnp.float32,
    )
    rows = len(pairs) * PAIR
    out = []
    for row in range(N_TM):
        total = None
        for m in range(RADIX):
            lanes = slice(row * LANES, (row + 1) * LANES)
            at = row % 2 * LANES
            re = spread[m * rows : (m + 1) * rows, at : at + LANES]
            im = spread[m * rows : (m + 1) * rows, POINTS + at : POINTS + at + LANES]
            term = re * outer[m : m + 1, lanes] - im * outer[RADIX + m : RADIX + m + 1, lanes]
            total = term if total is None else total + term
        out.append(total)
    return [
        [total[place * PAIR : (place + 1) * PAIR, :] for total in out] for place in range(len(pairs))
    ]


def kernel(
    chips, samples_ref, owner_ref, twiddle_ref, dft_ref, share_ref, inner_ref, outer_ref, out_ref,
    samples, twiddle, dft, share, inner, outer, owner, z, y, rows, white, cross, result,
    from_a, from_x, from_b, from_y,
    load_sem, send_sem, recv_sem, sum_send, sum_recv, ready, ready_two,
):
    position, t = lax.axis_index("chan"), lax.axis_index("tm")
    q, e = position // 2, lax.rem(position, 2)
    after, before = lax.rem(q + 1, chips), lax.rem(q + chips - 1, chips)

    def device(chip, core, row):
        return (chip * 2 + core, row)

    def other(step):
        return lax.rem(t + step, N_TM)

    barrier = pltpu.get_barrier_semaphore()

    def greet(target):
        pl.semaphore_signal(barrier, inc=1, device_id=target, device_id_type=MESH)

    last = q // (chips - 1)
    column = lax.rem(q, ROW)
    has_before, has_after = q > 0, last == 0
    opens, closes = column == 0, column == ROW - 1
    joins = jnp.logical_and(closes, has_after)
    lends = jnp.logical_and(column == 1, q > ROW)
    two_before, two_after = lax.rem(q + chips - 2, chips), lax.rem(q + 2, chips)

    @pl.when(has_before)
    def _():
        greet(device(before, e, t))

    @pl.when(lends)
    def _():
        greet(device(two_before, e, t))

    greet(device(q, 1 - e, t))
    for step in range(1, N_TM):
        for core in (0, 1):
            greet(device(q, core, other(step)))

    loads = [
        pltpu.make_async_copy(src, dst, load_sem.at[n])
        for n, (src, dst) in enumerate(
            [(samples_ref, samples), (twiddle_ref, twiddle), (dft_ref, dft), (share_ref, share),
             (inner_ref, inner), (outer_ref, outer), (owner_ref, owner)]
        )
    ]
    for load in loads:
        load.start()
    pl.semaphore_wait(barrier, 1 + 2 * (N_TM - 1) + (1 - last) * (1 + column // (ROW - 1)))

    def tell(semaphore, target):
        pl.semaphore_signal(semaphore, inc=1, device_id=target, device_id_type=MESH)

    @pl.when(has_after)
    def _():
        tell(ready, device(after, e, t))

    @pl.when(joins)
    def _():
        tell(ready_two, device(two_after, e, t))

    for load in loads[:4]:
        load.wait()

    whiten(samples, twiddle, dft, share, z, y, rows)
    own = pl.ds(pl.multiple_of(e * BLOCK, BLOCK), BLOCK)
    white[own, :] = rows[...].astype(jnp.bfloat16)

    def send(slot, n, target):
        place = pl.ds(pl.multiple_of(slot * BLOCK, BLOCK), BLOCK)
        return pltpu.make_async_remote_copy(
            src_ref=white.at[own, :], dst_ref=white.at[place, :], send_sem=send_sem.at[n],
            recv_sem=recv_sem.at[n], device_id=target, device_id_type=MESH,
        )

    to_after = send(2 + e, 1, device(after, e, t))
    to_other = send(e, 2, device(q, 1 - e, t))
    to_before = send(4, 0, device(before, e, t))
    to_two_before = send(5, 4, device(two_before, e, t))
    passed = pl.ds(3 * BLOCK, BLOCK)
    pass_on = pltpu.make_async_remote_copy(
        src_ref=white.at[passed, :], dst_ref=white.at[passed, :], send_sem=send_sem.at[3],
        recv_sem=recv_sem.at[3], device_id=device(q, 1 - e, t), device_id_type=MESH,
    )

    def put(place, value):
        for row in range(N_TM):
            result[row, place * PAIR : (place + 1) * PAIR, :] = value[row]

    def chosen(by, yes, no):
        return [jnp.where(by, a, b) for a, b in zip(yes, no)]

    def lagged(*pairs):
        return pair_lags(white, pairs, cross, inner, outer)

    def hand(core, step, n):
        row = other(step)
        near, far = n < 2, n < 4
        if core == 0:
            place, size, buffer, kind = n, 1, (from_a if near else from_b), (0 if near else 2)
        else:
            place, size = (0, 1, 3, 3, 4, 4)[n], 2 if near else 1
            buffer, kind = (from_x if near else from_y), (1 if near else 3)
        return pltpu.make_async_remote_copy(
            src_ref=result.at[row, pl.ds(place * PAIR, size * PAIR), :],
            dst_ref=buffer.at[t],
            send_sem=sum_send.at[step, n],
            recv_sem=sum_recv.at[kind, t],
            device_id=device(before if far and not near else q, n % 2, row),
            device_id_type=MESH,
        )

    def hands(core, targets):
        return [
            hand(core, step, n)
            for step in (2, 1, 3, 0)
            for n in targets
            if step > 0 or n % 2 != core or 2 <= n < 4
        ]

    def start(copies):
        for copy in copies:
            copy.start()
        return copies

    loads[4].wait()
    loads[5].wait()
    loads[6].wait()
    swap = owner[2 * q] != 2 * q
    swap_before = owner[2 * before] != 2 * before

    def first_core():
        @pl.when(has_before)
        def _():
            @pl.when(opens)
            def _():
                to_after.start()

            pl.semaphore_wait(ready, 1)
            to_before.start()

        to_other.start()

        @pl.when(jnp.logical_not(jnp.logical_or(closes, jnp.logical_and(opens, has_before))))
        def _():
            to_after.start()

        to_other.wait_recv()

        @pl.when(has_after)
        def _():
            to_before.wait_recv()

        one, two = lagged((0, 4), (1, 4))
        put(0, chosen(swap, two, one))
        put(1, chosen(swap, one, two))
        near = start(hands(0, (0, 1)))
        from_a[t] = result[t, :PAIR, :]

        @pl.when(jnp.logical_not(opens))
        def _():
            to_after.wait_recv()
            pass_on.wait_recv()
            one, two = lagged((2, 4), (3, 4))
            put(2, chosen(swap_before, two, one))
            put(3, chosen(swap_before, one, two))
            start(hands(0, (2, 3)))

        @pl.when(joins)
        def _():
            to_two_before.wait_recv()
            one, two = lagged((0, 5), (1, 5))
            put(4, chosen(swap, two, one))
            put(5, chosen(swap, one, two))
            start(hands(0, (4, 5)))
            from_b[t] = result[t, 4 * PAIR : 5 * PAIR, :]

        return near

    def second_core():
        @pl.when(jnp.logical_not(closes))
        def _():
            to_after.start()

        to_other.start()

        @pl.when(has_before)
        def _():
            pl.semaphore_wait(ready, 1)
            to_before.start()

        to_other.wait_recv()
        put(1, lagged((0, 1))[0])

        @pl.when(jnp.logical_not(opens))
        def _():
            to_after.wait_recv()
            pass_on.start()

        @pl.when(has_after)
        def _():
            to_before.wait_recv()

        @pl.when(jnp.logical_not(opens))
        def _():
            put(3, lagged((3, 4))[0])
            start(hands(1, (2, 3)))

        one, two = lagged((0, 4), (1, 4))
        put(0, chosen(swap, two, one))
        put(2, chosen(swap, one, two))
        near = start(hands(1, (0, 1)))
        from_x[t] = result[t, PAIR : 3 * PAIR, :]

        @pl.when(joins)
        def _():
            to_two_before.wait_recv()
            put(4, lagged((1, 5))[0])
            start(hands(1, (4, 5)))
            from_y[t] = result[t, 4 * PAIR : 5 * PAIR, :]

        return near

    for core, run in ((0, first_core), (1, second_core)):

        @pl.when(e == core)
        def _():
            near = run()

            @pl.when(lends)
            def _():
                pl.semaphore_wait(ready_two, 1)
                to_two_before.start()

            for copy in near:
                copy.wait_send()

            @pl.when(jnp.logical_not(opens))
            def _():
                for copy in hands(core, (2, 3)):
                    copy.wait_send()

            @pl.when(joins)
            def _():
                for copy in hands(core, (4, 5)):
                    copy.wait_send()

    def arrived(size, buffer, n, row):
        return pltpu.make_async_remote_copy(
            src_ref=result.at[0, pl.ds(0, size), :], dst_ref=buffer.at[row],
            send_sem=sum_send.at[0, n], recv_sem=sum_recv.at[n, row],
            device_id=device(q, 1 - e, t), device_id_type=MESH,
        )

    for step in range(N_TM):
        row = other(step)
        if step > 0:
            arrived(PAIR, from_a, 0, row).wait_recv()
            arrived(2 * PAIR, from_x, 1, row).wait_recv()

    @pl.when(has_after)
    def _():
        for step in range(1, N_TM):
            arrived(PAIR, from_b, 2, other(step)).wait_recv()
            arrived(PAIR, from_y, 3, other(step)).wait_recv()

    @pl.when(jnp.logical_or(jnp.logical_not(closes), jnp.logical_and(joins, e == 1)))
    def _():
        arrived(PAIR, from_b, 2, t).wait_recv()

    @pl.when(jnp.logical_or(jnp.logical_not(closes), jnp.logical_and(joins, e == 0)))
    def _():
        arrived(PAIR, from_y, 3, t).wait_recv()

    @pl.when(e == 1)
    def _():
        arrived(PAIR, from_a, 0, t).wait_recv()

    @pl.when(e == 0)
    def _():
        arrived(2 * PAIR, from_x, 1, t).wait_recv()

    def summed(buffer):
        return (buffer[0] + buffer[1]) + (buffer[2] + buffer[3])

    a, x, b, last = summed(from_a), summed(from_x), summed(from_b), summed(from_y)
    flip = e == 1
    right = jnp.where(flip, x[PAIR:], x[:PAIR])
    inner = jnp.where(flip, x[:PAIR], x[PAIR:])
    odd = jnp.logical_xor(swap, e == 1)
    block = 2 * q + odd.astype(jnp.int32)
    low = [inner, a, right, b]
    high = [a, right, b, last]
    for n in range(BAND):
        value = jnp.where(odd, high[n], low[n])
        out_ref[n * PAIR : (n + 1) * PAIR, :] = jnp.where(
            block + n + 1 < 2 * chips, value, jnp.zeros_like(value)
        )

    to_other.wait_send()

    @pl.when(has_before)
    def _():
        to_before.wait_send()

    @pl.when(lends)
    def _():
        to_two_before.wait_send()

    @pl.when(jnp.logical_not(closes))
    def _():
        to_after.wait_send()

    @pl.when(jnp.logical_and(e == 1, jnp.logical_not(opens)))
    def _():
        pass_on.wait_send()


def shards(chips, samples, block_owner):
    segments = samples.shape[1] * N_TM
    twiddle, dft, share, inner, outer = tables(segments)
    stay = pl.BlockSpec(memory_space=pltpu.HBM)
    out = pl.pallas_call(
        functools.partial(kernel, chips),
        out_shape=jax.ShapeDtypeStruct((BAND * PAIR, LANES), jnp.float32),
        in_specs=[stay] * 7,
        out_specs=pl.BlockSpec(memory_space=pltpu.VMEM),
        scratch_shapes=[
            pltpu.VMEM((CH, SEG, NSEG), jnp.float32),
            pltpu.VMEM(twiddle.shape, jnp.float32),
            pltpu.VMEM(dft.shape, jnp.float32),
            pltpu.VMEM(share.shape, jnp.float32),
            pltpu.VMEM(inner.shape, jnp.bfloat16),
            pltpu.VMEM(outer.shape, jnp.float32),
            pltpu.SMEM(block_owner.shape, jnp.int32),
            pltpu.VMEM((RADIX * ROWS, 2 * POINTS), jnp.float32),
            pltpu.VMEM((RADIX * ROWS, 2 * LANES), jnp.float32),
            pltpu.VMEM((BLOCK, LANES), jnp.float32),
            pltpu.VMEM((6 * BLOCK, LANES), jnp.bfloat16),
            pltpu.VMEM((4 * PAIR * RADIX, LANES), jnp.float32),
            pltpu.VMEM((N_TM, 6 * PAIR, LANES), jnp.float32),
            pltpu.VMEM((N_TM, PAIR, LANES), jnp.float32),
            pltpu.VMEM((N_TM, 2 * PAIR, LANES), jnp.float32),
            pltpu.VMEM((N_TM, PAIR, LANES), jnp.float32),
            pltpu.VMEM((N_TM, PAIR, LANES), jnp.float32),
            pltpu.SemaphoreType.DMA((7,)),
            pltpu.SemaphoreType.DMA((5,)),
            pltpu.SemaphoreType.DMA((5,)),
            pltpu.SemaphoreType.DMA((N_TM, 6)),
            pltpu.SemaphoreType.DMA((4, N_TM)),
            pltpu.SemaphoreType.REGULAR,
            pltpu.SemaphoreType.REGULAR,
        ],
        compiler_params=pltpu.CompilerParams(collective_id=0, has_side_effects=True),
    )(
        samples, block_owner, jnp.asarray(twiddle), jnp.asarray(dft), jnp.asarray(share),
        jnp.asarray(inner), jnp.asarray(outer),
    )
    return out.reshape(1, BAND, CH, CH, LANES)


def solution(mesh):
    in_specs = (P("chan", "tm", None), P())
    out_specs = P("chan", None, None, None, "tm")
    chips = mesh.shape["chan"] // 2
    return jax.shard_map(
        functools.partial(shards, chips), mesh=mesh, in_specs=in_specs, out_specs=out_specs,
        check_vma=False,
    )
```

```python
import functools
import math

import jax
import jax.numpy as jnp
import ml_dtypes
import numpy as np
from jax import lax
from jax.experimental import pallas as pl
from jax.experimental.pallas import tpu as pltpu
from jax.sharding import PartitionSpec as P

MESH = pl.DeviceIdType.MESH
NSEG = 2048
LAGS = 512
SMOOTH = 32
BAND = 4
NF = 1024
EPSILON = 1e-06
CH = 4
SEG = 8
ROWS = CH * SEG
LANES = 128
TILE = 16
RADIX = 8
POINTS = NSEG // RADIX
BLOCK = ROWS * TILE
HALF = BLOCK // 2
PAIR = CH * CH
N_TM = 4
ROW = 8


def tables(segments):
    t2 = np.arange(POINTS)
    radix = np.arange(RADIX)
    angle = 2.0 * math.pi * (radix[:, None] * t2[None, :] % NSEG) / NSEG
    twiddle = np.concatenate([np.cos(angle), np.sin(angle)], 0).astype(np.float32)
    angle = 2.0 * math.pi * (t2[:, None] * np.arange(LANES)[None, :] % POINTS) / POINTS
    cos, sin = np.cos(angle), np.sin(angle)
    dft = np.concatenate(
        [np.concatenate([cos, -sin], 1), np.concatenate([sin, cos], 1)], 0
    ).astype(np.float32)
    bins = radix[:, None] + RADIX * np.arange(LANES)[None, :]
    count = np.minimum(bins, SMOOTH) + np.minimum(NF - 1 - bins, SMOOTH) + 1
    share = (1.0 / count).astype(np.float32)
    angle = 2.0 * math.pi * (np.arange(LANES)[:, None] * np.arange(POINTS)[None, :] % POINTS) / POINTS
    cos, sin = np.cos(angle), np.sin(angle)
    inner = np.concatenate([np.concatenate([cos, sin], 1), np.concatenate([-sin, cos], 1)], 0)
    lag = np.arange(LAGS) - LAGS // 2
    angle = 2.0 * math.pi * (radix[:, None] * lag[None, :] % NSEG) / NSEG
    factor = 1.0 / (math.sqrt(NF) * segments)
    outer = np.concatenate([np.cos(angle), np.sin(angle)], 0) * factor
    return twiddle, dft, share, inner.astype(ml_dtypes.bfloat16), outer.astype(np.float32)


def shifted(x, by):
    lane = lax.broadcasted_iota(jnp.int32, x.shape, 1)
    if by > 0:
        return jnp.where(lane >= by, pltpu.roll(x, by, 1), 0.0)
    return jnp.where(lane < LANES + by, pltpu.roll(x, LANES + by, 1), 0.0)


def radix_stage(x, twiddle):
    c = math.sqrt(0.5)
    a0, b0 = x[0] + x[4], x[0] - x[4]
    a1, b1 = x[1] + x[5], x[1] - x[5]
    a2, b2 = x[2] + x[6], x[2] - x[6]
    a3, b3 = x[3] + x[7], x[3] - x[7]
    even, odd = a0 + a2, a1 + a3
    low, high = c * (b1 - b3), c * (b1 + b3)
    y = [
        (even + odd, None),
        (b0 + low, -(b2 + high)),
        (a0 - a2, a3 - a1),
        (b0 - low, b2 - high),
        (even - odd, None),
    ]
    y += [(y[3][0], -y[3][1]), (y[2][0], -y[2][1]), (y[1][0], -y[1][1])]
    out = []
    for k1, (re, im) in enumerate(y):
        cos, sin = twiddle[k1 : k1 + 1, :], twiddle[RADIX + k1 : RADIX + k1 + 1, :]
        if k1 == 0:
            out.append((re, jnp.zeros_like(re)))
        elif im is None:
            out.append((re * cos, -(re * sin)))
        else:
            out.append((re * cos + im * sin, im * cos - re * sin))
    return out


def whiten(samples, twiddle, dft, share, z, y, rows, first, channels):
    size = channels * SEG
    x = [
        samples[first : first + channels, :, t * POINTS : (t + 1) * POINTS].reshape(size, POINTS)
        for t in range(RADIX)
    ]
    total = ((x[0] + x[1]) + (x[2] + x[3])) + ((x[4] + x[5]) + (x[6] + x[7]))
    mean = jnp.sum(total, axis=1, keepdims=True) * (1.0 / NSEG)
    x = [part - mean for part in x]
    for k1, (re, im) in enumerate(radix_stage(x, twiddle)):
        z[k1 * size : (k1 + 1) * size, :POINTS] = re
        z[k1 * size : (k1 + 1) * size, POINTS:] = im
    spectra = slice(0, RADIX * size)
    y[spectra, :] = jnp.dot(
        z[spectra, :], dft[...], precision=lax.Precision.HIGHEST, preferred_element_type=jnp.float32
    )
    re = [y[m * size : (m + 1) * size, :LANES] for m in range(RADIX)]
    im = [y[m * size : (m + 1) * size, LANES:] for m in range(RADIX)]
    length = [jnp.sqrt(r * r + i * i) for r, i in zip(re, im)]
    before, after = [length[0]], [length[-1]]
    for m in range(1, RADIX):
        before.append(before[-1] + length[m])
        after.append(after[-1] + length[RADIX - 1 - m])
    after = after[::-1]
    whole = before[-1]
    middle = whole
    for by in (1, 2, 3):
        middle = middle + (shifted(whole, by) + shifted(whole, -by))
    for m in range(RADIX):
        window = middle + (shifted(before[m], -4) + shifted(after[m], 4))
        scale = 1.0 / (window * share[m : m + 1, :] + EPSILON)
        start = first * SEG * TILE + m
        rows[pl.ds(start, size, stride=TILE), :] = re[m] * scale
        rows[pl.ds(start + RADIX, size, stride=TILE), :] = im[m] * scale


def pair_cross(white, left, right, cross, place):
    def body(s, total):
        def halves(slot, channel):
            start = pl.multiple_of(slot * BLOCK + (channel * SEG + s) * TILE, TILE)
            tile = white[pl.ds(start, TILE), :].astype(jnp.float32)
            return tile[:RADIX, :], tile[RADIX:, :]

        lefts = [halves(left, i) for i in range(CH)]
        rights = [halves(right, j) for j in range(CH)]
        out = []
        for i in range(CH):
            for j in range(CH):
                (lr, li), (rr, ri) = lefts[i], rights[j]
                re, im = total[2 * (i * CH + j)], total[2 * (i * CH + j) + 1]
                out.append(re + (lr * rr + li * ri))
                out.append(im + (li * rr - lr * ri))
        return tuple(out)

    zero = jnp.zeros((RADIX, LANES), jnp.float32)
    total = lax.fori_loop(0, SEG, body, (zero,) * (2 * PAIR), unroll=True)
    for p in range(PAIR):
        for part in (0, 1):
            start = ((2 * place + part) * PAIR + p) * RADIX
            cross[start : start + RADIX, :] = total[2 * p + part]


def pair_lags(white, pairs, cross, inner, outer):
    for place, (left, right) in enumerate(pairs):
        pair_cross(white, left, right, cross, place)
    parts = []
    for part in (0, 1):
        rows = [
            cross[pl.ds((2 * place + part) * PAIR * RADIX + m, PAIR, stride=RADIX), :]
            for m in range(RADIX)
            for place in range(len(pairs))
        ]
        parts.append(jnp.concatenate(rows, axis=0))
    spread = jnp.dot(
        jnp.concatenate(parts, axis=1).astype(jnp.bfloat16),
        inner[...],
        preferred_element_type=jnp.float32,
    )
    rows = len(pairs) * PAIR
    out = []
    for row in range(N_TM):
        total = None
        for m in range(RADIX):
            lanes = slice(row * LANES, (row + 1) * LANES)
            at = row % 2 * LANES
            re = spread[m * rows : (m + 1) * rows, at : at + LANES]
            im = spread[m * rows : (m + 1) * rows, POINTS + at : POINTS + at + LANES]
            term = re * outer[m : m + 1, lanes] - im * outer[RADIX + m : RADIX + m + 1, lanes]
            total = term if total is None else total + term
        out.append(total)
    return [
        [total[place * PAIR : (place + 1) * PAIR, :] for total in out] for place in range(len(pairs))
    ]


def kernel(
    chips, samples_ref, owner_ref, twiddle_ref, dft_ref, share_ref, inner_ref, outer_ref, out_ref,
    samples, twiddle, dft, share, inner, outer, owner, z, y, rows, white, cross, result,
    from_a, from_x, from_b, from_y,
    load_sem, send_sem, recv_sem, sum_send, sum_recv, ready, ready_two,
):
    position, t = lax.axis_index("chan"), lax.axis_index("tm")
    q, e = position // 2, lax.rem(position, 2)
    after, before = lax.rem(q + 1, chips), lax.rem(q + chips - 1, chips)

    def device(chip, core, row):
        return (chip * 2 + core, row)

    def other(step):
        return lax.rem(t + step, N_TM)

    loads = [
        pltpu.make_async_copy(src, dst, load_sem.at[n])
        for n, (src, dst) in enumerate(
            [(samples_ref, samples), (twiddle_ref, twiddle), (dft_ref, dft), (share_ref, share),
             (inner_ref, inner), (outer_ref, outer), (owner_ref, owner)]
        )
    ]
    for load in loads:
        load.start()

    barrier = pltpu.get_barrier_semaphore()

    def greet(target):
        pl.semaphore_signal(barrier, inc=1, device_id=target, device_id_type=MESH)

    last = q // (chips - 1)
    column = lax.rem(q, ROW)
    has_before, has_after = q > 0, last == 0
    opens, closes = column == 0, column == ROW - 1
    joins = jnp.logical_and(closes, has_after)
    lends = jnp.logical_and(column == 1, q > ROW)
    two_before, two_after = lax.rem(q + chips - 2, chips), lax.rem(q + 2, chips)

    @pl.when(has_before)
    def _():
        greet(device(before, e, t))

    @pl.when(lends)
    def _():
        greet(device(two_before, e, t))

    greet(device(q, 1 - e, t))
    for step in range(1, N_TM):
        for core in (0, 1):
            greet(device(q, core, other(step)))

    pl.semaphore_wait(barrier, 1 + 2 * (N_TM - 1) + (1 - last) * (1 + column // (ROW - 1)))

    def tell(semaphore, target):
        pl.semaphore_signal(semaphore, inc=1, device_id=target, device_id_type=MESH)

    @pl.when(has_after)
    def _():
        tell(ready, device(after, e, t))

    @pl.when(joins)
    def _():
        tell(ready_two, device(two_after, e, t))

    for load in loads[:4]:
        load.wait()

    class Halves:
        def __init__(self, source, slot, n, target):
            self.copies = []
            for half in (0, 1):
                start = pl.multiple_of(source * BLOCK + half * HALF, HALF)
                place = pl.multiple_of(slot * BLOCK + half * HALF, HALF)
                self.copies.append(
                    pltpu.make_async_remote_copy(
                        src_ref=white.at[pl.ds(start, HALF), :],
                        dst_ref=white.at[pl.ds(place, HALF), :],
                        send_sem=send_sem.at[n, half],
                        recv_sem=recv_sem.at[n, half],
                        device_id=target,
                        device_id_type=MESH,
                    )
                )

        def start(self):
            for copy in self.copies:
                copy.start()

        def wait_recv(self):
            for copy in self.copies:
                copy.wait_recv()

        def wait_send(self):
            for copy in self.copies:
                copy.wait_send()

    to_after = Halves(e, 2 + e, 1, device(after, e, t))
    to_other = Halves(e, e, 2, device(q, 1 - e, t))
    to_before = Halves(e, 4, 0, device(before, e, t))
    to_two_before = Halves(e, 5, 4, device(two_before, e, t))
    pass_on = Halves(3, 3, 3, device(q, 1 - e, t))

    def ahead(half):
        @pl.when(jnp.logical_not(closes))
        def _():
            to_after.copies[half].start()

    def back(half):
        @pl.when(jnp.logical_not(opens))
        def _():
            if half == 0:
                pl.semaphore_wait(ready, 1)
            to_before.copies[half].start()

    for half in (0, 1):
        whiten(samples, twiddle, dft, share, z, y, rows, half * CH // 2, CH // 2)
        start = pl.multiple_of(e * BLOCK + half * HALF, HALF)
        white[pl.ds(start, HALF), :] = rows[half * HALF : (half + 1) * HALF, :].astype(jnp.bfloat16)

        @pl.when(e == 0)
        def _():
            back(half)
            ahead(half)

        @pl.when(e == 1)
        def _():
            ahead(half)
            back(half)

        to_other.copies[half].start()

    @pl.when(jnp.logical_and(opens, has_before))
    def _():
        pl.semaphore_wait(ready, 1)
        to_before.start()

    def put(place, value):
        for row in range(N_TM):
            result[row, place * PAIR : (place + 1) * PAIR, :] = value[row].astype(jnp.bfloat16)

    def chosen(by, yes, no):
        return [jnp.where(by, a, b) for a, b in zip(yes, no)]

    def lagged(*pairs):
        return pair_lags(white, pairs, cross, inner, outer)

    def hand(core, step, n):
        row = other(step)
        near, far = n < 2, n < 4
        if core == 0:
            place, size, buffer, kind = n, 1, (from_a if near else from_b), (0 if near else 2)
        else:
            place, size = (0, 1, 3, 3, 4, 4)[n], 2 if near else 1
            buffer, kind = (from_x if near else from_y), (1 if near else 3)
        return pltpu.make_async_remote_copy(
            src_ref=result.at[row, pl.ds(place * PAIR, size * PAIR), :],
            dst_ref=buffer.at[t],
            send_sem=sum_send.at[step, n],
            recv_sem=sum_recv.at[kind, t],
            device_id=device(before if far and not near else q, n % 2, row),
            device_id_type=MESH,
        )

    def hands(core, targets):
        return [
            hand(core, step, n)
            for step in (2, 1, 3, 0)
            for n in targets
            if step > 0 or n % 2 != core or 2 <= n < 4
        ]

    def start(copies):
        for copy in copies:
            copy.start()
        return copies

    loads[4].wait()
    loads[5].wait()
    loads[6].wait()
    swap = owner[2 * q] != 2 * q
    swap_before = owner[2 * before] != 2 * before

    def first_core():
        to_other.wait_recv()

        @pl.when(has_after)
        def _():
            to_before.wait_recv()

        @pl.when(jnp.logical_not(opens))
        def _():
            to_after.wait_recv()
            pass_on.wait_recv()
            one, two = lagged((2, 4), (3, 4))
            put(2, chosen(swap_before, two, one))
            put(3, chosen(swap_before, one, two))
            start(hands(0, (2, 3)))

        one, two = lagged((0, 4), (1, 4))
        put(0, chosen(swap, two, one))
        put(1, chosen(swap, one, two))
        near = start(hands(0, (0, 1)))
        from_a[t] = result[t, :PAIR, :]

        @pl.when(joins)
        def _():
            to_two_before.wait_recv()
            one, two = lagged((0, 5), (1, 5))
            put(4, chosen(swap, two, one))
            put(5, chosen(swap, one, two))
            start(hands(0, (4, 5)))
            from_b[t] = result[t, 4 * PAIR : 5 * PAIR, :]

        return near

    def second_core():
        to_other.wait_recv()
        put(1, lagged((0, 1))[0])

        @pl.when(jnp.logical_not(opens))
        def _():
            for copy, passed in zip(to_after.copies, pass_on.copies):
                copy.wait_recv()
                passed.start()

        @pl.when(has_after)
        def _():
            to_before.wait_recv()

        @pl.when(jnp.logical_not(opens))
        def _():
            put(3, lagged((3, 4))[0])
            start(hands(1, (2, 3)))

        one, two = lagged((0, 4), (1, 4))
        put(0, chosen(swap, two, one))
        put(2, chosen(swap, one, two))
        near = start(hands(1, (0, 1)))
        from_x[t] = result[t, PAIR : 3 * PAIR, :]

        @pl.when(joins)
        def _():
            to_two_before.wait_recv()
            put(4, lagged((1, 5))[0])
            start(hands(1, (4, 5)))
            from_y[t] = result[t, 4 * PAIR : 5 * PAIR, :]

        return near

    for core, run in ((0, first_core), (1, second_core)):

        @pl.when(e == core)
        def _():
            near = run()

            @pl.when(lends)
            def _():
                pl.semaphore_wait(ready_two, 1)
                to_two_before.start()

            for copy in near:
                copy.wait_send()

            @pl.when(jnp.logical_not(opens))
            def _():
                for copy in hands(core, (2, 3)):
                    copy.wait_send()

            @pl.when(joins)
            def _():
                for copy in hands(core, (4, 5)):
                    copy.wait_send()

    def arrived(size, buffer, n, row):
        return pltpu.make_async_remote_copy(
            src_ref=result.at[0, pl.ds(0, size), :], dst_ref=buffer.at[row],
            send_sem=sum_send.at[0, n], recv_sem=sum_recv.at[n, row],
            device_id=device(q, 1 - e, t), device_id_type=MESH,
        )

    for step in range(N_TM):
        row = other(step)
        if step > 0:
            arrived(PAIR, from_a, 0, row).wait_recv()
            arrived(2 * PAIR, from_x, 1, row).wait_recv()

    @pl.when(has_after)
    def _():
        for step in range(1, N_TM):
            arrived(PAIR, from_b, 2, other(step)).wait_recv()
            arrived(PAIR, from_y, 3, other(step)).wait_recv()

    @pl.when(jnp.logical_or(jnp.logical_not(closes), jnp.logical_and(joins, e == 1)))
    def _():
        arrived(PAIR, from_b, 2, t).wait_recv()

    @pl.when(jnp.logical_or(jnp.logical_not(closes), jnp.logical_and(joins, e == 0)))
    def _():
        arrived(PAIR, from_y, 3, t).wait_recv()

    @pl.when(e == 1)
    def _():
        arrived(PAIR, from_a, 0, t).wait_recv()

    @pl.when(e == 0)
    def _():
        arrived(2 * PAIR, from_x, 1, t).wait_recv()

    def summed(buffer):
        first, second, third, fourth = [buffer[row].astype(jnp.float32) for row in range(N_TM)]
        return (first + second) + (third + fourth)

    a, x, b, last = summed(from_a), summed(from_x), summed(from_b), summed(from_y)
    flip = e == 1
    right = jnp.where(flip, x[PAIR:], x[:PAIR])
    inner = jnp.where(flip, x[:PAIR], x[PAIR:])
    odd = jnp.logical_xor(swap, e == 1)
    block = 2 * q + odd.astype(jnp.int32)
    low = [inner, a, right, b]
    high = [a, right, b, last]
    for n in range(BAND):
        value = jnp.where(odd, high[n], low[n])
        out_ref[n * PAIR : (n + 1) * PAIR, :] = jnp.where(
            block + n + 1 < 2 * chips, value, jnp.zeros_like(value)
        )

    to_other.wait_send()

    @pl.when(has_before)
    def _():
        to_before.wait_send()

    @pl.when(lends)
    def _():
        to_two_before.wait_send()

    @pl.when(jnp.logical_not(closes))
    def _():
        to_after.wait_send()

    @pl.when(jnp.logical_and(e == 1, jnp.logical_not(opens)))
    def _():
        pass_on.wait_send()


def shards(chips, samples, block_owner):
    segments = samples.shape[1] * N_TM
    twiddle, dft, share, inner, outer = tables(segments)
    stay = pl.BlockSpec(memory_space=pltpu.HBM)
    out = pl.pallas_call(
        functools.partial(kernel, chips),
        out_shape=pltpu.VMEM((BAND * PAIR, LANES), jnp.float32),
        in_specs=[stay] * 7,
        out_specs=pl.BlockSpec(memory_space=pltpu.VMEM),
        scratch_shapes=[
            pltpu.VMEM((CH, SEG, NSEG), jnp.float32),
            pltpu.VMEM(twiddle.shape, jnp.float32),
            pltpu.VMEM(dft.shape, jnp.float32),
            pltpu.VMEM(share.shape, jnp.float32),
            pltpu.VMEM(inner.shape, jnp.bfloat16),
            pltpu.VMEM(outer.shape, jnp.float32),
            pltpu.SMEM(block_owner.shape, jnp.int32),
            pltpu.VMEM((RADIX * ROWS, 2 * POINTS), jnp.float32),
            pltpu.VMEM((RADIX * ROWS, 2 * LANES), jnp.float32),
            pltpu.VMEM((BLOCK, LANES), jnp.float32),
            pltpu.VMEM((6 * BLOCK, LANES), jnp.bfloat16),
            pltpu.VMEM((4 * PAIR * RADIX, LANES), jnp.float32),
            pltpu.VMEM((N_TM, 6 * PAIR, LANES), jnp.bfloat16),
            pltpu.VMEM((N_TM, PAIR, LANES), jnp.bfloat16),
            pltpu.VMEM((N_TM, 2 * PAIR, LANES), jnp.bfloat16),
            pltpu.VMEM((N_TM, PAIR, LANES), jnp.bfloat16),
            pltpu.VMEM((N_TM, PAIR, LANES), jnp.bfloat16),
            pltpu.SemaphoreType.DMA((7,)),
            pltpu.SemaphoreType.DMA((5, 2)),
            pltpu.SemaphoreType.DMA((5, 2)),
            pltpu.SemaphoreType.DMA((N_TM, 6)),
            pltpu.SemaphoreType.DMA((4, N_TM)),
            pltpu.SemaphoreType.REGULAR,
            pltpu.SemaphoreType.REGULAR,
        ],
        compiler_params=pltpu.CompilerParams(
            collective_id=0, has_side_effects=True, vmem_limit_bytes=58 * 1024 * 1024
        ),
    )(
        samples, block_owner, jnp.asarray(twiddle), jnp.asarray(dft), jnp.asarray(share),
        jnp.asarray(inner), jnp.asarray(outer),
    )
    return out.reshape(1, BAND, CH, CH, LANES)


def solution(mesh):
    in_specs = (P("chan", "tm", None), P())
    out_specs = P("chan", None, None, None, "tm")
    chips = mesh.shape["chan"] // 2
    return jax.shard_map(
        functools.partial(shards, chips), mesh=mesh, in_specs=in_specs, out_specs=out_specs,
        check_vma=False,
    )
```

```python
import functools
import math

import jax
import jax.numpy as jnp
import ml_dtypes
import numpy as np
from jax import lax
from jax.experimental import pallas as pl
from jax.experimental.pallas import tpu as pltpu
from jax.sharding import PartitionSpec as P

MESH = pl.DeviceIdType.MESH
NSEG = 2048
LAGS = 512
SMOOTH = 32
BAND = 4
NF = 1024
EPSILON = 1e-06
CH = 4
SEG = 8
ROWS = CH * SEG
LANES = 128
TILE = 16
RADIX = 8
POINTS = NSEG // RADIX
BLOCK = ROWS * TILE
HALF = BLOCK // 2
PAIR = CH * CH
N_TM = 4
ROW = 8


def tables(segments):
    t2 = np.arange(POINTS)
    radix = np.arange(RADIX)
    angle = 2.0 * math.pi * (radix[:, None] * t2[None, :] % NSEG) / NSEG
    twiddle = np.concatenate([np.cos(angle), np.sin(angle)], 0).astype(np.float32)
    angle = 2.0 * math.pi * (t2[:, None] * np.arange(LANES)[None, :] % POINTS) / POINTS
    cos, sin = np.cos(angle), np.sin(angle)
    dft = np.concatenate(
        [np.concatenate([cos, -sin], 1), np.concatenate([sin, cos], 1)], 0
    ).astype(np.float32)
    bins = radix[:, None] + RADIX * np.arange(LANES)[None, :]
    count = np.minimum(bins, SMOOTH) + np.minimum(NF - 1 - bins, SMOOTH) + 1
    share = (1.0 / count).astype(np.float32)
    angle = 2.0 * math.pi * (np.arange(LANES)[:, None] * np.arange(POINTS)[None, :] % POINTS) / POINTS
    cos, sin = np.cos(angle), np.sin(angle)
    inner = np.concatenate([np.concatenate([cos, sin], 1), np.concatenate([-sin, cos], 1)], 0)
    lag = np.arange(LAGS) - LAGS // 2
    angle = 2.0 * math.pi * (radix[:, None] * lag[None, :] % NSEG) / NSEG
    factor = 1.0 / (math.sqrt(NF) * segments)
    outer = np.concatenate([np.cos(angle), np.sin(angle)], 0) * factor
    return twiddle, dft, share, inner.astype(ml_dtypes.bfloat16), outer.astype(np.float32)


def shifted(x, by):
    lane = lax.broadcasted_iota(jnp.int32, x.shape, 1)
    if by > 0:
        return jnp.where(lane >= by, pltpu.roll(x, by, 1), 0.0)
    return jnp.where(lane < LANES + by, pltpu.roll(x, LANES + by, 1), 0.0)


def radix_stage(x, twiddle):
    c = math.sqrt(0.5)
    a0, b0 = x[0] + x[4], x[0] - x[4]
    a1, b1 = x[1] + x[5], x[1] - x[5]
    a2, b2 = x[2] + x[6], x[2] - x[6]
    a3, b3 = x[3] + x[7], x[3] - x[7]
    even, odd = a0 + a2, a1 + a3
    low, high = c * (b1 - b3), c * (b1 + b3)
    y = [
        (even + odd, None),
        (b0 + low, -(b2 + high)),
        (a0 - a2, a3 - a1),
        (b0 - low, b2 - high),
        (even - odd, None),
    ]
    y += [(y[3][0], -y[3][1]), (y[2][0], -y[2][1]), (y[1][0], -y[1][1])]
    out = []
    for k1, (re, im) in enumerate(y):
        cos, sin = twiddle[k1 : k1 + 1, :], twiddle[RADIX + k1 : RADIX + k1 + 1, :]
        if k1 == 0:
            out.append((re, jnp.zeros_like(re)))
        elif im is None:
            out.append((re * cos, -(re * sin)))
        else:
            out.append((re * cos + im * sin, im * cos - re * sin))
    return out


def whiten(samples, twiddle, dft, share, z, y, rows, first, channels):
    size = channels * SEG
    x = [
        samples[first : first + channels, :, t * POINTS : (t + 1) * POINTS].reshape(size, POINTS)
        for t in range(RADIX)
    ]
    total = ((x[0] + x[1]) + (x[2] + x[3])) + ((x[4] + x[5]) + (x[6] + x[7]))
    mean = jnp.sum(total, axis=1, keepdims=True) * (1.0 / NSEG)
    x = [part - mean for part in x]
    for k1, (re, im) in enumerate(radix_stage(x, twiddle)):
        z[k1 * size : (k1 + 1) * size, :POINTS] = re
        z[k1 * size : (k1 + 1) * size, POINTS:] = im
    spectra = slice(0, RADIX * size)
    y[spectra, :] = jnp.dot(
        z[spectra, :], dft[...], precision=lax.Precision.HIGHEST, preferred_element_type=jnp.float32
    )
    re = [y[m * size : (m + 1) * size, :LANES] for m in range(RADIX)]
    im = [y[m * size : (m + 1) * size, LANES:] for m in range(RADIX)]
    length = [jnp.sqrt(r * r + i * i) for r, i in zip(re, im)]
    before, after = [length[0]], [length[-1]]
    for m in range(1, RADIX):
        before.append(before[-1] + length[m])
        after.append(after[-1] + length[RADIX - 1 - m])
    after = after[::-1]
    whole = before[-1]
    middle = whole
    for by in (1, 2, 3):
        middle = middle + (shifted(whole, by) + shifted(whole, -by))
    for m in range(RADIX):
        window = middle + (shifted(before[m], -4) + shifted(after[m], 4))
        scale = 1.0 / (window * share[m : m + 1, :] + EPSILON)
        start = first * SEG * TILE + m
        rows[pl.ds(start, size, stride=TILE), :] = re[m] * scale
        rows[pl.ds(start + RADIX, size, stride=TILE), :] = im[m] * scale


def pair_cross(white, left, right, cross, place):
    def body(s, total):
        def halves(slot, channel):
            start = pl.multiple_of(slot * BLOCK + (channel * SEG + s) * TILE, TILE)
            tile = white[pl.ds(start, TILE), :].astype(jnp.float32)
            return tile[:RADIX, :], tile[RADIX:, :]

        lefts = [halves(left, i) for i in range(CH)]
        rights = [halves(right, j) for j in range(CH)]
        out = []
        for i in range(CH):
            for j in range(CH):
                (lr, li), (rr, ri) = lefts[i], rights[j]
                re, im = total[2 * (i * CH + j)], total[2 * (i * CH + j) + 1]
                out.append(re + (lr * rr + li * ri))
                out.append(im + (li * rr - lr * ri))
        return tuple(out)

    zero = jnp.zeros((RADIX, LANES), jnp.float32)
    total = lax.fori_loop(0, SEG, body, (zero,) * (2 * PAIR), unroll=True)
    for p in range(PAIR):
        for part in (0, 1):
            start = ((2 * place + part) * PAIR + p) * RADIX
            cross[start : start + RADIX, :] = total[2 * p + part]


def pair_lags(white, pairs, cross, inner, outer):
    for place, (left, right) in enumerate(pairs):
        pair_cross(white, left, right, cross, place)
    parts = []
    for part in (0, 1):
        rows = [
            cross[pl.ds((2 * place + part) * PAIR * RADIX + m, PAIR, stride=RADIX), :]
            for m in range(RADIX)
            for place in range(len(pairs))
        ]
        parts.append(jnp.concatenate(rows, axis=0))
    spread = jnp.dot(
        jnp.concatenate(parts, axis=1).astype(jnp.bfloat16),
        inner[...],
        preferred_element_type=jnp.float32,
    )
    rows = len(pairs) * PAIR
    out = []
    for row in range(N_TM):
        total = None
        for m in range(RADIX):
            lanes = slice(row * LANES, (row + 1) * LANES)
            at = row % 2 * LANES
            re = spread[m * rows : (m + 1) * rows, at : at + LANES]
            im = spread[m * rows : (m + 1) * rows, POINTS + at : POINTS + at + LANES]
            term = re * outer[m : m + 1, lanes] - im * outer[RADIX + m : RADIX + m + 1, lanes]
            total = term if total is None else total + term
        out.append(total)
    return [
        [total[place * PAIR : (place + 1) * PAIR, :] for total in out] for place in range(len(pairs))
    ]


def kernel(
    chips, samples_ref, owner_ref, twiddle_ref, dft_ref, share_ref, inner_ref, outer_ref, out_ref,
    samples, twiddle, dft, share, inner, outer, owner, z, y, rows, white, cross, result,
    from_a, from_x, from_b, from_y,
    load_sem, send_sem, recv_sem, sum_send, sum_recv, ready, ready_back, ready_two,
):
    position, t = lax.axis_index("chan"), lax.axis_index("tm")
    q, e = position // 2, lax.rem(position, 2)
    after, before = lax.rem(q + 1, chips), lax.rem(q + chips - 1, chips)

    def device(chip, core, row):
        return (chip * 2 + core, row)

    def other(step):
        return lax.rem(t + step, N_TM)

    loads = [
        pltpu.make_async_copy(src, dst, load_sem.at[n])
        for n, (src, dst) in enumerate(
            [(samples_ref, samples), (twiddle_ref, twiddle), (dft_ref, dft), (share_ref, share),
             (inner_ref, inner), (outer_ref, outer), (owner_ref, owner)]
        )
    ]
    for load in loads:
        load.start()

    barrier = pltpu.get_barrier_semaphore()

    def greet(target):
        pl.semaphore_signal(barrier, inc=1, device_id=target, device_id_type=MESH)

    last = q // (chips - 1)
    column = lax.rem(q, ROW)
    has_before, has_after = q > 0, last == 0
    opens, closes = column == 0, column == ROW - 1
    first = q == 0
    joins = jnp.logical_and(closes, has_after)
    lends = jnp.logical_and(column == 1, q > ROW)
    two_before, two_after = lax.rem(q + chips - 2, chips), lax.rem(q + 2, chips)

    @pl.when(jnp.logical_not(closes))
    def _():
        greet(device(after, e, t))

    @pl.when(jnp.logical_and(opens, has_before))
    def _():
        greet(device(before, e, t))

    @pl.when(lends)
    def _():
        greet(device(two_before, e, t))

    greet(device(q, 1 - e, t))
    for step in range(1, N_TM):
        for core in (0, 1):
            greet(device(q, core, other(step)))

    in_row, at_end = (column + ROW - 1) // ROW, column // (ROW - 1)
    pl.semaphore_wait(barrier, 1 + 2 * (N_TM - 1) + in_row + 2 * (1 - last) * at_end)

    def tell(semaphore, target):
        pl.semaphore_signal(semaphore, inc=1, device_id=target, device_id_type=MESH)

    @pl.when(jnp.logical_not(opens))
    def _():
        tell(ready, device(before, e, t))

    @pl.when(joins)
    def _():
        tell(ready_back, device(after, e, t))
        tell(ready_two, device(two_after, e, t))

    for load in loads[:4]:
        load.wait()

    class Halves:
        def __init__(self, source, slot, n, target):
            self.copies = []
            for half in (0, 1):
                start = pl.multiple_of(source * BLOCK + half * HALF, HALF)
                place = pl.multiple_of(slot * BLOCK + half * HALF, HALF)
                self.copies.append(
                    pltpu.make_async_remote_copy(
                        src_ref=white.at[pl.ds(start, HALF), :],
                        dst_ref=white.at[pl.ds(place, HALF), :],
                        send_sem=send_sem.at[n, half],
                        recv_sem=recv_sem.at[n, half],
                        device_id=target,
                        device_id_type=MESH,
                    )
                )

        def start(self):
            for copy in self.copies:
                copy.start()

        def wait_recv(self):
            for copy in self.copies:
                copy.wait_recv()

        def wait_send(self):
            for copy in self.copies:
                copy.wait_send()

    to_after = Halves(e, 2 + e, 1, device(after, e, t))
    to_other = Halves(e, e, 2, device(q, 1 - e, t))
    to_before = Halves(e, 4, 0, device(before, e, t))
    to_two_before = Halves(e, 5, 4, device(two_before, e, t))
    pass_on = Halves(3, 3, 3, device(q, 1 - e, t))

    for half in (0, 1):
        whiten(samples, twiddle, dft, share, z, y, rows, half * CH // 2, CH // 2)
        start = pl.multiple_of(e * BLOCK + half * HALF, HALF)
        white[pl.ds(start, HALF), :] = rows[half * HALF : (half + 1) * HALF, :].astype(jnp.bfloat16)

        @pl.when(jnp.logical_not(opens))
        def _():
            to_before.copies[half].start()

        @pl.when(first)
        def _():
            if half == 0:
                pl.semaphore_wait(ready, 1)
            to_after.copies[half].start()

    @pl.when(jnp.logical_not(jnp.logical_or(first, closes)))
    def _():
        pl.semaphore_wait(ready, 1)
        to_after.start()

    to_other.start()

    @pl.when(jnp.logical_and(opens, has_before))
    def _():
        pl.semaphore_wait(ready_back, 1)
        to_before.start()

    def put(place, value):
        for row in range(N_TM):
            result[row, place * PAIR : (place + 1) * PAIR, :] = value[row].astype(jnp.bfloat16)

    def chosen(by, yes, no):
        return [jnp.where(by, a, b) for a, b in zip(yes, no)]

    def lagged(*pairs):
        return pair_lags(white, pairs, cross, inner, outer)

    def hand(core, step, n):
        row = other(step)
        near, far = n < 2, n < 4
        if core == 0:
            place, size, buffer, kind = n, 1, (from_a if near else from_b), (0 if near else 2)
        else:
            place, size = (0, 1, 3, 3, 4, 4)[n], 2 if near else 1
            buffer, kind = (from_x if near else from_y), (1 if near else 3)
        return pltpu.make_async_remote_copy(
            src_ref=result.at[row, pl.ds(place * PAIR, size * PAIR), :],
            dst_ref=buffer.at[t],
            send_sem=sum_send.at[step, n],
            recv_sem=sum_recv.at[kind],
            device_id=device(before if far and not near else q, n % 2, row),
            device_id_type=MESH,
        )

    def each_hand(core, targets, act):
        @pl.loop(0, N_TM - 1)
        def _(turn):
            for n in targets:
                act(hand(core, 1 + lax.rem(turn + 1, N_TM - 1), n))

        for n in targets:
            if n % 2 != core or 2 <= n < 4:
                act(hand(core, 0, n))

    def start(core, targets):
        each_hand(core, targets, lambda copy: copy.start())

    def finish(core, targets):
        each_hand(core, targets, lambda copy: copy.wait_send())

    def keep(buffer, kind, place, size):
        rows_kept = pl.ds(place * PAIR, size * PAIR)
        pltpu.make_async_copy(result.at[t, rows_kept, :], buffer.at[t], sum_recv.at[kind]).start()

    loads[4].wait()
    loads[5].wait()
    loads[6].wait()
    swap = owner[2 * q] != 2 * q
    swap_before = owner[2 * before] != 2 * before

    def first_core():
        to_other.wait_recv()

        @pl.when(has_after)
        def _():
            to_before.wait_recv()

        @pl.when(jnp.logical_not(opens))
        def _():
            to_after.wait_recv()
            pass_on.wait_recv()
            one, two = lagged((2, 4), (3, 4))
            put(2, chosen(swap_before, two, one))
            put(3, chosen(swap_before, one, two))
            start(0, (2, 3))

        one, two = lagged((0, 4), (1, 4))
        put(0, chosen(swap, two, one))
        put(1, chosen(swap, one, two))
        start(0, (0, 1))
        keep(from_a, 0, 0, 1)

        @pl.when(joins)
        def _():
            to_two_before.wait_recv()
            one, two = lagged((0, 5), (1, 5))
            put(4, chosen(swap, two, one))
            put(5, chosen(swap, one, two))
            start(0, (4, 5))
            keep(from_b, 2, 4, 1)

    def second_core():
        to_other.wait_recv()
        put(1, lagged((0, 1))[0])

        @pl.when(jnp.logical_not(opens))
        def _():
            for copy, passed in zip(to_after.copies, pass_on.copies):
                copy.wait_recv()
                passed.start()

        @pl.when(has_after)
        def _():
            to_before.wait_recv()

        @pl.when(jnp.logical_not(opens))
        def _():
            put(3, lagged((3, 4))[0])
            start(1, (2, 3))

        one, two = lagged((0, 4), (1, 4))
        put(0, chosen(swap, two, one))
        put(2, chosen(swap, one, two))
        start(1, (0, 1))
        keep(from_x, 1, 1, 2)

        @pl.when(joins)
        def _():
            to_two_before.wait_recv()
            put(4, lagged((1, 5))[0])
            start(1, (4, 5))
            keep(from_y, 3, 4, 1)

    for core, run in ((0, first_core), (1, second_core)):

        @pl.when(e == core)
        def _():
            run()

            @pl.when(lends)
            def _():
                pl.semaphore_wait(ready_two, 1)
                to_two_before.start()

            finish(core, (0, 1))

            @pl.when(jnp.logical_not(opens))
            def _():
                finish(core, (2, 3))

            @pl.when(joins)
            def _():
                finish(core, (4, 5))

    to_other.wait_send()

    @pl.when(has_before)
    def _():
        to_before.wait_send()

    @pl.when(lends)
    def _():
        to_two_before.wait_send()

    @pl.when(jnp.logical_not(closes))
    def _():
        to_after.wait_send()

    @pl.when(jnp.logical_and(e == 1, jnp.logical_not(opens)))
    def _():
        pass_on.wait_send()

    def arrived(buffer, kind):
        pltpu.make_async_copy(buffer, buffer, sum_recv.at[kind]).wait()

    arrived(from_a, 0)
    arrived(from_x, 1)

    @pl.when(has_after)
    def _():
        arrived(from_b, 2)
        arrived(from_y, 3)

    def summed(buffer):
        first, second, third, fourth = [buffer[row].astype(jnp.float32) for row in range(N_TM)]
        return (first + second) + (third + fourth)

    a, x, b, last = summed(from_a), summed(from_x), summed(from_b), summed(from_y)
    flip = e == 1
    right = jnp.where(flip, x[PAIR:], x[:PAIR])
    inner = jnp.where(flip, x[:PAIR], x[PAIR:])
    odd = jnp.logical_xor(swap, e == 1)
    block = 2 * q + odd.astype(jnp.int32)
    low = [inner, a, right, b]
    high = [a, right, b, last]
    for n in range(BAND):
        value = jnp.where(odd, high[n], low[n])
        out_ref[n * PAIR : (n + 1) * PAIR, :] = jnp.where(
            block + n + 1 < 2 * chips, value, jnp.zeros_like(value)
        )


def shards(chips, samples, block_owner):
    segments = samples.shape[1] * N_TM
    twiddle, dft, share, inner, outer = tables(segments)
    stay = pl.BlockSpec(memory_space=pltpu.HBM)
    out = pl.pallas_call(
        functools.partial(kernel, chips),
        out_shape=pltpu.VMEM((BAND * PAIR, LANES), jnp.float32),
        in_specs=[stay] * 7,
        out_specs=pl.BlockSpec(memory_space=pltpu.VMEM),
        scratch_shapes=[
            pltpu.VMEM((CH, SEG, NSEG), jnp.float32),
            pltpu.VMEM(twiddle.shape, jnp.float32),
            pltpu.VMEM(dft.shape, jnp.float32),
            pltpu.VMEM(share.shape, jnp.float32),
            pltpu.VMEM(inner.shape, jnp.bfloat16),
            pltpu.VMEM(outer.shape, jnp.float32),
            pltpu.SMEM(block_owner.shape, jnp.int32),
            pltpu.VMEM((RADIX * ROWS, 2 * POINTS), jnp.float32),
            pltpu.VMEM((RADIX * ROWS, 2 * LANES), jnp.float32),
            pltpu.VMEM((BLOCK, LANES), jnp.float32),
            pltpu.VMEM((6 * BLOCK, LANES), jnp.bfloat16),
            pltpu.VMEM((4 * PAIR * RADIX, LANES), jnp.float32),
            pltpu.VMEM((N_TM, 6 * PAIR, LANES), jnp.bfloat16),
            pltpu.VMEM((N_TM, PAIR, LANES), jnp.bfloat16),
            pltpu.VMEM((N_TM, 2 * PAIR, LANES), jnp.bfloat16),
            pltpu.VMEM((N_TM, PAIR, LANES), jnp.bfloat16),
            pltpu.VMEM((N_TM, PAIR, LANES), jnp.bfloat16),
            pltpu.SemaphoreType.DMA((7,)),
            pltpu.SemaphoreType.DMA((5, 2)),
            pltpu.SemaphoreType.DMA((5, 2)),
            pltpu.SemaphoreType.DMA((N_TM, 6)),
            pltpu.SemaphoreType.DMA((4,)),
            pltpu.SemaphoreType.REGULAR,
            pltpu.SemaphoreType.REGULAR,
            pltpu.SemaphoreType.REGULAR,
        ],
        compiler_params=pltpu.CompilerParams(
            collective_id=0, has_side_effects=True, vmem_limit_bytes=58 * 1024 * 1024
        ),
    )(
        samples, block_owner, jnp.asarray(twiddle), jnp.asarray(dft), jnp.asarray(share),
        jnp.asarray(inner), jnp.asarray(outer),
    )
    return out.reshape(1, BAND, CH, CH, LANES)


def solution(mesh):
    in_specs = (P("chan", "tm", None), P())
    out_specs = P("chan", None, None, None, "tm")
    chips = mesh.shape["chan"] // 2
    return jax.shard_map(
        functools.partial(shards, chips), mesh=mesh, in_specs=in_specs, out_specs=out_specs,
        check_vma=False,
    )
```

```python
import functools
import math

import jax
import jax.numpy as jnp
import ml_dtypes
import numpy as np
from jax import lax
from jax.experimental import pallas as pl
from jax.experimental.pallas import tpu as pltpu
from jax.sharding import PartitionSpec as P

MESH = pl.DeviceIdType.MESH
NSEG = 2048
LAGS = 512
SMOOTH = 32
BAND = 4
NF = 1024
EPSILON = 1e-06
CH = 4
SEG = 8
ROWS = CH * SEG
LANES = 128
TILE = 16
RADIX = 8
POINTS = NSEG // RADIX
BLOCK = ROWS * TILE
HALF = BLOCK // 2
PAIR = CH * CH
N_TM = 4
ROW = 8


def tables(segments):
    t2 = np.arange(POINTS)
    radix = np.arange(RADIX)
    angle = 2.0 * math.pi * (radix[:, None] * t2[None, :] % NSEG) / NSEG
    twiddle = np.concatenate([np.cos(angle), np.sin(angle)], 0).astype(np.float32)
    angle = 2.0 * math.pi * (t2[:, None] * np.arange(LANES)[None, :] % POINTS) / POINTS
    cos, sin = np.cos(angle), np.sin(angle)
    dft = np.concatenate(
        [np.concatenate([cos, -sin], 1), np.concatenate([sin, cos], 1)], 0
    ).astype(np.float32)
    bins = radix[:, None] + RADIX * np.arange(LANES)[None, :]
    count = np.minimum(bins, SMOOTH) + np.minimum(NF - 1 - bins, SMOOTH) + 1
    share = (1.0 / count).astype(np.float32)
    angle = 2.0 * math.pi * (np.arange(LANES)[:, None] * np.arange(POINTS)[None, :] % POINTS) / POINTS
    cos, sin = np.cos(angle), np.sin(angle)
    inner = np.concatenate([np.concatenate([cos, sin], 1), np.concatenate([-sin, cos], 1)], 0)
    lag = np.arange(LAGS) - LAGS // 2
    angle = 2.0 * math.pi * (radix[:, None] * lag[None, :] % NSEG) / NSEG
    factor = 1.0 / (math.sqrt(NF) * segments)
    outer = np.concatenate([np.cos(angle), np.sin(angle)], 0) * factor
    return twiddle, dft, share, inner.astype(ml_dtypes.bfloat16), outer.astype(np.float32)


def shifted(x, by):
    lane = lax.broadcasted_iota(jnp.int32, x.shape, 1)
    if by > 0:
        return jnp.where(lane >= by, pltpu.roll(x, by, 1), 0.0)
    return jnp.where(lane < LANES + by, pltpu.roll(x, LANES + by, 1), 0.0)


def radix_stage(x, twiddle):
    c = math.sqrt(0.5)
    a0, b0 = x[0] + x[4], x[0] - x[4]
    a1, b1 = x[1] + x[5], x[1] - x[5]
    a2, b2 = x[2] + x[6], x[2] - x[6]
    a3, b3 = x[3] + x[7], x[3] - x[7]
    even, odd = a0 + a2, a1 + a3
    low, high = c * (b1 - b3), c * (b1 + b3)
    y = [
        (even + odd, None),
        (b0 + low, -(b2 + high)),
        (a0 - a2, a3 - a1),
        (b0 - low, b2 - high),
        (even - odd, None),
    ]
    y += [(y[3][0], -y[3][1]), (y[2][0], -y[2][1]), (y[1][0], -y[1][1])]
    out = []
    for k1, (re, im) in enumerate(y):
        cos, sin = twiddle[k1 : k1 + 1, :], twiddle[RADIX + k1 : RADIX + k1 + 1, :]
        if k1 == 0:
            out.append((re, jnp.zeros_like(re)))
        elif im is None:
            out.append((re * cos, -(re * sin)))
        else:
            out.append((re * cos + im * sin, im * cos - re * sin))
    return out


def whiten(samples, twiddle, dft, share, z, y, rows, first, channels):
    size = channels * SEG
    x = [
        samples[first : first + channels, :, t * POINTS : (t + 1) * POINTS].reshape(size, POINTS)
        for t in range(RADIX)
    ]
    total = ((x[0] + x[1]) + (x[2] + x[3])) + ((x[4] + x[5]) + (x[6] + x[7]))
    mean = jnp.sum(total, axis=1, keepdims=True) * (1.0 / NSEG)
    x = [part - mean for part in x]
    for k1, (re, im) in enumerate(radix_stage(x, twiddle)):
        z[k1 * size : (k1 + 1) * size, :POINTS] = re
        z[k1 * size : (k1 + 1) * size, POINTS:] = im
    spectra = slice(0, RADIX * size)
    y[spectra, :] = jnp.dot(
        z[spectra, :], dft[...], precision=lax.Precision.HIGHEST, preferred_element_type=jnp.float32
    )
    re = [y[m * size : (m + 1) * size, :LANES] for m in range(RADIX)]
    im = [y[m * size : (m + 1) * size, LANES:] for m in range(RADIX)]
    length = [jnp.sqrt(r * r + i * i) for r, i in zip(re, im)]
    before, after = [length[0]], [length[-1]]
    for m in range(1, RADIX):
        before.append(before[-1] + length[m])
        after.append(after[-1] + length[RADIX - 1 - m])
    after = after[::-1]
    whole = before[-1]
    middle = whole
    for by in (1, 2, 3):
        middle = middle + (shifted(whole, by) + shifted(whole, -by))
    for m in range(RADIX):
        window = middle + (shifted(before[m], -4) + shifted(after[m], 4))
        scale = 1.0 / (window * share[m : m + 1, :] + EPSILON)
        start = first * SEG * TILE + m
        rows[pl.ds(start, size, stride=TILE), :] = re[m] * scale
        rows[pl.ds(start + RADIX, size, stride=TILE), :] = im[m] * scale


def pair_cross(white, left, right, cross, place):
    def body(s, total):
        def halves(slot, channel):
            start = pl.multiple_of(slot * BLOCK + (channel * SEG + s) * TILE, TILE)
            tile = white[pl.ds(start, TILE), :].astype(jnp.float32)
            return tile[:RADIX, :], tile[RADIX:, :]

        lefts = [halves(left, i) for i in range(CH)]
        rights = [halves(right, j) for j in range(CH)]
        out = []
        for i in range(CH):
            for j in range(CH):
                (lr, li), (rr, ri) = lefts[i], rights[j]
                re, im = total[2 * (i * CH + j)], total[2 * (i * CH + j) + 1]
                out.append(re + (lr * rr + li * ri))
                out.append(im + (li * rr - lr * ri))
        return tuple(out)

    zero = jnp.zeros((RADIX, LANES), jnp.float32)
    total = lax.fori_loop(0, SEG, body, (zero,) * (2 * PAIR), unroll=True)
    for p in range(PAIR):
        for part in (0, 1):
            start = ((2 * place + part) * PAIR + p) * RADIX
            cross[start : start + RADIX, :] = total[2 * p + part]


def pair_lags(white, pairs, cross, inner, outer):
    for place, (left, right) in enumerate(pairs):
        pair_cross(white, left, right, cross, place)
    parts = []
    for part in (0, 1):
        rows = [
            cross[pl.ds((2 * place + part) * PAIR * RADIX + m, PAIR, stride=RADIX), :]
            for m in range(RADIX)
            for place in range(len(pairs))
        ]
        parts.append(jnp.concatenate(rows, axis=0))
    spread = jnp.dot(
        jnp.concatenate(parts, axis=1).astype(jnp.bfloat16),
        inner[...],
        preferred_element_type=jnp.float32,
    )
    rows = len(pairs) * PAIR
    out = []
    for row in range(N_TM):
        total = None
        for m in range(RADIX):
            lanes = slice(row * LANES, (row + 1) * LANES)
            at = row % 2 * LANES
            re = spread[m * rows : (m + 1) * rows, at : at + LANES]
            im = spread[m * rows : (m + 1) * rows, POINTS + at : POINTS + at + LANES]
            term = re * outer[m : m + 1, lanes] - im * outer[RADIX + m : RADIX + m + 1, lanes]
            total = term if total is None else total + term
        out.append(total)
    return [
        [total[place * PAIR : (place + 1) * PAIR, :] for total in out] for place in range(len(pairs))
    ]


def kernel(
    chips, samples_ref, owner_ref, twiddle_ref, dft_ref, share_ref, inner_ref, outer_ref, out_ref,
    samples, twiddle, dft, share, inner, outer, owner, z, y, rows, white, cross, result,
    from_a, from_x, from_b, from_y,
    load_sem, send_sem, recv_sem, sum_send, sum_recv, ready, ready_back, ready_two,
):
    position, t = lax.axis_index("chan"), lax.axis_index("tm")
    q, e = position // 2, lax.rem(position, 2)
    after, before = lax.rem(q + 1, chips), lax.rem(q + chips - 1, chips)

    def device(chip, core, row):
        return (chip * 2 + core, row)

    def other(step):
        return lax.rem(t + step, N_TM)

    loads = [
        pltpu.make_async_copy(src, dst, load_sem.at[n])
        for n, (src, dst) in enumerate(
            [(samples_ref, samples), (twiddle_ref, twiddle), (dft_ref, dft), (share_ref, share),
             (inner_ref, inner), (outer_ref, outer), (owner_ref, owner)]
        )
    ]
    for load in loads:
        load.start()

    barrier = pltpu.get_barrier_semaphore()

    def greet(target):
        pl.semaphore_signal(barrier, inc=1, device_id=target, device_id_type=MESH)

    last = q // (chips - 1)
    column = lax.rem(q, ROW)
    has_before, has_after = q > 0, last == 0
    opens, closes = column == 0, column == ROW - 1
    first = q == 0
    joins = jnp.logical_and(closes, has_after)
    lends = jnp.logical_and(column == 1, q > ROW)
    two_before, two_after = lax.rem(q + chips - 2, chips), lax.rem(q + 2, chips)

    second = q == 1
    held = jnp.logical_or(second, jnp.logical_and(opens, has_before))

    @pl.when(jnp.logical_not(jnp.logical_or(first, closes)))
    def _():
        greet(device(after, e, t))

    @pl.when(held)
    def _():
        greet(device(before, e, t))

    @pl.when(lends)
    def _():
        greet(device(two_before, e, t))

    greet(device(q, 1 - e, t))
    for step in range(1, N_TM):
        for core in (0, 1):
            greet(device(q, core, other(step)))

    in_row, at_end = (column + ROW - 1) // ROW, column // (ROW - 1)
    is_first = (chips - 1 - q) // (chips - 1)
    in_row += is_first - ((chips - q) // (chips - 1) - is_first)
    pl.semaphore_wait(barrier, 1 + 2 * (N_TM - 1) + in_row + 2 * (1 - last) * at_end)

    def tell(semaphore, target):
        pl.semaphore_signal(semaphore, inc=1, device_id=target, device_id_type=MESH)

    in_line = jnp.logical_not(jnp.logical_or(opens, second))

    @pl.when(in_line)
    def _():
        tell(ready, device(before, e, t))

    @pl.when(jnp.logical_or(first, joins))
    def _():
        tell(ready_back, device(after, e, t))

    @pl.when(joins)
    def _():
        tell(ready_two, device(two_after, e, t))

    for load in loads[:4]:
        load.wait()

    class Halves:
        def __init__(self, source, slot, n, target):
            self.copies = []
            for half in (0, 1):
                start = pl.multiple_of(source * BLOCK + half * HALF, HALF)
                place = pl.multiple_of(slot * BLOCK + half * HALF, HALF)
                self.copies.append(
                    pltpu.make_async_remote_copy(
                        src_ref=white.at[pl.ds(start, HALF), :],
                        dst_ref=white.at[pl.ds(place, HALF), :],
                        send_sem=send_sem.at[n, half],
                        recv_sem=recv_sem.at[n, half],
                        device_id=target,
                        device_id_type=MESH,
                    )
                )

        def start(self):
            for copy in self.copies:
                copy.start()

        def wait_recv(self):
            for copy in self.copies:
                copy.wait_recv()

        def wait_send(self):
            for copy in self.copies:
                copy.wait_send()

    to_after = Halves(e, 2 + e, 1, device(after, e, t))
    to_other = Halves(e, e, 2, device(q, 1 - e, t))
    to_before = Halves(e, 4, 0, device(before, e, t))
    to_two_before = Halves(e, 5, 4, device(two_before, e, t))
    pass_on = Halves(3, 3, 3, device(q, 1 - e, t))

    for half in (0, 1):
        whiten(samples, twiddle, dft, share, z, y, rows, half * CH // 2, CH // 2)
        start = pl.multiple_of(e * BLOCK + half * HALF, HALF)
        white[pl.ds(start, HALF), :] = rows[half * HALF : (half + 1) * HALF, :].astype(jnp.bfloat16)

        @pl.when(in_line)
        def _():
            to_before.copies[half].start()

        @pl.when(first)
        def _():
            to_after.copies[half].start()

    @pl.when(jnp.logical_not(jnp.logical_or(first, closes)))
    def _():
        pl.semaphore_wait(ready, 1)
        to_after.start()

    to_other.start()

    @pl.when(held)
    def _():
        pl.semaphore_wait(ready_back, 1)
        to_before.start()

    def put(place, value):
        for row in range(N_TM):
            result[row, place * PAIR : (place + 1) * PAIR, :] = value[row].astype(jnp.bfloat16)

    def chosen(by, yes, no):
        return [jnp.where(by, a, b) for a, b in zip(yes, no)]

    def lagged(*pairs):
        return pair_lags(white, pairs, cross, inner, outer)

    def hand(core, step, n):
        row = other(step)
        near, far = n < 2, n < 4
        if core == 0:
            place, size, buffer, kind = n, 1, (from_a if near else from_b), (0 if near else 2)
        else:
            place, size = (0, 1, 3, 3, 4, 4)[n], 2 if near else 1
            buffer, kind = (from_x if near else from_y), (1 if near else 3)
        return pltpu.make_async_remote_copy(
            src_ref=result.at[row, pl.ds(place * PAIR, size * PAIR), :],
            dst_ref=buffer.at[t],
            send_sem=sum_send.at[step, n],
            recv_sem=sum_recv.at[kind],
            device_id=device(before if far and not near else q, n % 2, row),
            device_id_type=MESH,
        )

    def each_hand(core, targets, act):
        @pl.loop(0, N_TM - 1)
        def _(turn):
            for n in targets:
                act(hand(core, 1 + lax.rem(turn + 1, N_TM - 1), n))

        for n in targets:
            if n % 2 != core or 2 <= n < 4:
                act(hand(core, 0, n))

    def start(core, targets):
        each_hand(core, targets, lambda copy: copy.start())

    def finish(core, targets):
        each_hand(core, targets, lambda copy: copy.wait_send())

    def keep(buffer, kind, place, size):
        rows_kept = pl.ds(place * PAIR, size * PAIR)
        pltpu.make_async_copy(result.at[t, rows_kept, :], buffer.at[t], sum_recv.at[kind]).start()

    loads[4].wait()
    loads[5].wait()
    loads[6].wait()
    swap = owner[2 * q] != 2 * q
    swap_before = owner[2 * before] != 2 * before

    def first_core():
        to_other.wait_recv()

        @pl.when(has_after)
        def _():
            to_before.wait_recv()

        @pl.when(jnp.logical_not(opens))
        def _():
            to_after.wait_recv()
            pass_on.wait_recv()
            one, two = lagged((2, 4), (3, 4))
            put(2, chosen(swap_before, two, one))
            put(3, chosen(swap_before, one, two))
            start(0, (2, 3))

        one, two = lagged((0, 4), (1, 4))
        put(0, chosen(swap, two, one))
        put(1, chosen(swap, one, two))
        start(0, (0, 1))
        keep(from_a, 0, 0, 1)

        @pl.when(joins)
        def _():
            to_two_before.wait_recv()
            one, two = lagged((0, 5), (1, 5))
            put(4, chosen(swap, two, one))
            put(5, chosen(swap, one, two))
            start(0, (4, 5))
            keep(from_b, 2, 4, 1)

    def second_core():
        to_other.wait_recv()
        put(1, lagged((0, 1))[0])

        @pl.when(jnp.logical_not(opens))
        def _():
            for copy, passed in zip(to_after.copies, pass_on.copies):
                copy.wait_recv()
                passed.start()

        @pl.when(has_after)
        def _():
            to_before.wait_recv()

        @pl.when(jnp.logical_not(opens))
        def _():
            put(3, lagged((3, 4))[0])
            start(1, (2, 3))

        one, two = lagged((0, 4), (1, 4))
        put(0, chosen(swap, two, one))
        put(2, chosen(swap, one, two))
        start(1, (0, 1))
        keep(from_x, 1, 1, 2)

        @pl.when(joins)
        def _():
            to_two_before.wait_recv()
            put(4, lagged((1, 5))[0])
            start(1, (4, 5))
            keep(from_y, 3, 4, 1)

    for core, run in ((0, first_core), (1, second_core)):

        @pl.when(e == core)
        def _():
            run()

            @pl.when(lends)
            def _():
                pl.semaphore_wait(ready_two, 1)
                to_two_before.start()

            finish(core, (0, 1))

            @pl.when(jnp.logical_not(opens))
            def _():
                finish(core, (2, 3))

            @pl.when(joins)
            def _():
                finish(core, (4, 5))

    to_other.wait_send()

    @pl.when(has_before)
    def _():
        to_before.wait_send()

    @pl.when(lends)
    def _():
        to_two_before.wait_send()

    @pl.when(jnp.logical_not(closes))
    def _():
        to_after.wait_send()

    @pl.when(jnp.logical_and(e == 1, jnp.logical_not(opens)))
    def _():
        pass_on.wait_send()

    def arrived(buffer, kind):
        pltpu.make_async_copy(buffer, buffer, sum_recv.at[kind]).wait()

    arrived(from_a, 0)
    arrived(from_x, 1)

    @pl.when(has_after)
    def _():
        arrived(from_b, 2)
        arrived(from_y, 3)

    def summed(buffer):
        first, second, third, fourth = [buffer[row].astype(jnp.float32) for row in range(N_TM)]
        return (first + second) + (third + fourth)

    a, x, b, last = summed(from_a), summed(from_x), summed(from_b), summed(from_y)
    flip = e == 1
    right = jnp.where(flip, x[PAIR:], x[:PAIR])
    inner = jnp.where(flip, x[:PAIR], x[PAIR:])
    odd = jnp.logical_xor(swap, e == 1)
    block = 2 * q + odd.astype(jnp.int32)
    low = [inner, a, right, b]
    high = [a, right, b, last]
    for n in range(BAND):
        value = jnp.where(odd, high[n], low[n])
        out_ref[n * PAIR : (n + 1) * PAIR, :] = jnp.where(
            block + n + 1 < 2 * chips, value, jnp.zeros_like(value)
        )


def shards(chips, samples, block_owner):
    segments = samples.shape[1] * N_TM
    twiddle, dft, share, inner, outer = tables(segments)
    stay = pl.BlockSpec(memory_space=pltpu.HBM)
    out = pl.pallas_call(
        functools.partial(kernel, chips),
        out_shape=pltpu.VMEM((BAND * PAIR, LANES), jnp.float32),
        in_specs=[stay] * 7,
        out_specs=pl.BlockSpec(memory_space=pltpu.VMEM),
        scratch_shapes=[
            pltpu.VMEM((CH, SEG, NSEG), jnp.float32),
            pltpu.VMEM(twiddle.shape, jnp.float32),
            pltpu.VMEM(dft.shape, jnp.float32),
            pltpu.VMEM(share.shape, jnp.float32),
            pltpu.VMEM(inner.shape, jnp.bfloat16),
            pltpu.VMEM(outer.shape, jnp.float32),
            pltpu.SMEM(block_owner.shape, jnp.int32),
            pltpu.VMEM((RADIX * ROWS, 2 * POINTS), jnp.float32),
            pltpu.VMEM((RADIX * ROWS, 2 * LANES), jnp.float32),
            pltpu.VMEM((BLOCK, LANES), jnp.float32),
            pltpu.VMEM((6 * BLOCK, LANES), jnp.bfloat16),
            pltpu.VMEM((4 * PAIR * RADIX, LANES), jnp.float32),
            pltpu.VMEM((N_TM, 6 * PAIR, LANES), jnp.bfloat16),
            pltpu.VMEM((N_TM, PAIR, LANES), jnp.bfloat16),
            pltpu.VMEM((N_TM, 2 * PAIR, LANES), jnp.bfloat16),
            pltpu.VMEM((N_TM, PAIR, LANES), jnp.bfloat16),
            pltpu.VMEM((N_TM, PAIR, LANES), jnp.bfloat16),
            pltpu.SemaphoreType.DMA((7,)),
            pltpu.SemaphoreType.DMA((5, 2)),
            pltpu.SemaphoreType.DMA((5, 2)),
            pltpu.SemaphoreType.DMA((N_TM, 6)),
            pltpu.SemaphoreType.DMA((4,)),
            pltpu.SemaphoreType.REGULAR,
            pltpu.SemaphoreType.REGULAR,
            pltpu.SemaphoreType.REGULAR,
        ],
        compiler_params=pltpu.CompilerParams(
            collective_id=0, has_side_effects=True, vmem_limit_bytes=58 * 1024 * 1024
        ),
    )(
        samples, block_owner, jnp.asarray(twiddle), jnp.asarray(dft), jnp.asarray(share),
        jnp.asarray(inner), jnp.asarray(outer),
    )
    return out.reshape(1, BAND, CH, CH, LANES)


def solution(mesh):
    in_specs = (P("chan", "tm", None), P())
    out_specs = P("chan", None, None, None, "tm")
    chips = mesh.shape["chan"] // 2
    return jax.shard_map(
        functools.partial(shards, chips), mesh=mesh, in_specs=in_specs, out_specs=out_specs,
        check_vma=False,
    )
```
